128 devices in a mesh: row: 16 (over x, y), col: 8 (over z, core).
Axes of the slice: x: 4, y: 4, z: 4, core: 2. Of those that a mesh axis runs over, the one named last changes fastest.
Arguments:
- object_field: float32 [2, 8192, 4096], P(None, 'row', 'col'), may hold values from -6 to 6
- probe: bfloat16 [2, 4, 256, 256], replicated, may hold values from -3 to 3
- patterns: float32 [1024, 256, 256], P(('row', 'col')), may hold values from 0.3 to 4
- offsets: int32 [2, 1024], P(None, ('row', 'col')), may hold values from 0 to 7936, as said below
- counts: int32 [16, 8], P('row', 'col'), may hold values from 1 to 8, as said below
Outputs:
- object_grad: float32 [2, 8192, 4096], P(None, 'row', 'col')
- probe_grad: float32 [2, 4, 256, 256], replicated
The draws below stay inside these ranges and needn't reach their ends.
Inputs may be any that keep to these rules, and one draw needn't show every extreme that they name: `offsets`: the patch of a slot held by the device at (r, c) lies inside object rows r * 512 - 128 to (r + 1) * 512 + 128 and columns c * 512 - 128 to (c + 1) * 512 + 128, and inside the object. `counts`: some device has all 8 slots live.
All inputs are finite; a program needn't handle non-finite values.
Results may differ from the reference program's by a relative error of at most 0.005.
Values sent between devices are 32-bit elements; how exact they have to be, the bound alone decides.
No kernel may reach another device: no remote copies, remote signals or barrier semaphores. Data moves between devices by JAX's collectives and lax.ppermute only.
A program may use at most 128 MiB of HBM per device.

```python
import math
import jax
import jax.numpy as jnp
from jax import lax

PAT = 256
MODES = 4
TILE = 512
POS_DEV = 8
HALO = 128
OY = 8192
OX = 4096
NPOS = 1024
N_ROW = 16
N_COL = 8


def draw_counts(key, part):
    key = jax.random.fold_in(key, 11)
    first, second, third = jax.random.split(key, 3)
    total = N_ROW * N_COL
    upper = jax.random.randint(first, (total,), 1, POS_DEV + 1)
    values = jax.random.randint(second, (total,), 0, 1048576) % upper + 1
    chosen = jax.random.randint(third, (), 0, total)
    values = jnp.where(jnp.arange(total) == chosen, POS_DEV, values)
    return values.reshape(N_ROW, N_COL).astype(jnp.int32)


def corner_draw(key, tile_index, count):
    lower = jnp.where(tile_index == 0, 0, -HALO)
    upper = jnp.where(tile_index == count - 1, TILE - PAT, TILE - PAT + HALO)
    spread = jax.random.randint(key, (NPOS,), 0, 1048576) % (upper - lower + 1)
    return (lower, upper, lower + spread)


def draw_offsets(key, part):
    key = jax.random.fold_in(key, 23)
    keys = jax.random.split(key, 3)
    index = jnp.arange(NPOS)
    device = index // POS_DEV
    slot_number = index % POS_DEV
    row_index = device // N_COL
    col_index = device % N_COL
    low_row, high_row, local_row = corner_draw(keys[0], row_index, N_ROW)
    low_col, high_col, local_col = corner_draw(keys[1], col_index, N_COL)
    base = jax.random.randint(keys[2], (N_ROW * N_COL,), 0, POS_DEV)[device]
    picks = [(base + which) % POS_DEV for which in range(4)]
    local_row = jnp.where(slot_number == picks[0], low_row, local_row)
    local_row = jnp.where(slot_number == picks[1], high_row, local_row)
    local_col = jnp.where(slot_number == picks[2], low_col, local_col)
    local_col = jnp.where(slot_number == picks[3], high_col, local_col)
    rows_out = row_index * TILE + local_row
    cols_out = col_index * TILE + local_col
    return jnp.stack([rows_out, cols_out]).astype(jnp.int32)


def steps_of(key, dims, shards, least, largest):
    factor_of = 1.0
    for dim, parts in shards:
        heights = jax.random.uniform(jax.random.fold_in(jax.random.fold_in(key, 6), dim), (parts,), jnp.float32, least / len(shards), largest / len(shards))
        factor_of = factor_of * jnp.repeat(jnp.exp(heights), dims[dim] // parts).reshape((-1,) + (1,) * (len(dims) - 1 - dim))
    return factor_of


def centred(key, shape, width, most, cuts=(), kind=jnp.bfloat16):
    array = jax.random.normal(key, shape, jnp.float32) * width
    if len(cuts) > 0:
        array = steps_of(key, shape, cuts, -0.22, 0.18) * array
    return jnp.clip(array, min=-most, max=most).astype(kind)


def setup_inputs(seed: int = 0) -> dict:
    seeds = jax.random.split(jax.random.key(seed), 6)
    object_field = centred(seeds[0], (2, OY, OX), 1.0, 6.0, ((1, 16), (2, 8)), jnp.float32)
    probe = centred(seeds[1], (2, MODES, PAT, PAT), 0.5, 3.0)
    patterns = jnp.clip(jnp.exp(math.log(4.0) - 2.5902671 * jax.random.uniform(seeds[2], (NPOS, PAT, PAT), jnp.float32) ** steps_of(seeds[2], (NPOS, PAT, PAT), ((0, 128),), -0.2, 0.2)), 0.3, 4.0)
    offsets = draw_offsets(jax.random.fold_in(seeds[5], 71), 0)
    counts = draw_counts(jax.random.fold_in(seeds[5], 71), 0)
    return {"object_field": object_field, "probe": probe, "patterns": patterns, "offsets": offsets, "counts": counts}


def tables(length):
    index = jnp.arange(length, dtype=jnp.int32)
    product = index[:, None] * index[None, :] % length
    angle = product.astype(jnp.float32) * (2.0 * math.pi / length)
    factor = 1.0 / math.sqrt(length)
    return ((jnp.cos(angle) * factor).astype(jnp.bfloat16), (-jnp.sin(angle) * factor).astype(jnp.bfloat16))

def right_dot(matrix, table):
    return jnp.einsum('kab,bc->kac', matrix.astype(jnp.float32), table.astype(jnp.float32), precision=lax.Precision.HIGHEST)

def left_dot(table, matrix):
    return jnp.einsum('ab,kbc->kac', table.astype(jnp.float32), matrix.astype(jnp.float32), precision=lax.Precision.HIGHEST)

def right_mult(real_part, imag_part, table_re, table_im):
    return (right_dot(real_part, table_re) - right_dot(imag_part, table_im), right_dot(real_part, table_im) + right_dot(imag_part, table_re))

def left_mult(table_re, table_im, real_part, imag_part):
    return (left_dot(table_re, real_part) - left_dot(table_im, imag_part), left_dot(table_re, imag_part) + left_dot(table_im, real_part))

def position(patch_re, patch_im, measured, probe_re, probe_im, table_re, table_im):
    probe_fr = probe_re.astype(jnp.float32)
    probe_fi = probe_im.astype(jnp.float32)
    exit_re = (probe_fr * patch_re - probe_fi * patch_im).astype(jnp.bfloat16)
    exit_im = (probe_fr * patch_im + probe_fi * patch_re).astype(jnp.bfloat16)
    half_re, half_im = right_mult(exit_re, exit_im, table_re, table_im)
    field_re, field_im = left_mult(table_re, table_im, half_re.astype(jnp.bfloat16), half_im.astype(jnp.bfloat16))
    intensity = lax.optimization_barrier(jnp.sum(field_re * field_re + field_im * field_im, axis=0))
    amplitude = jnp.sqrt(jnp.maximum(intensity, 1.0))
    ratio = 1.0 - measured / amplitude
    resid_re = (field_re * ratio).astype(jnp.bfloat16)
    resid_im = (field_im * ratio).astype(jnp.bfloat16)
    conj_im = -table_im
    back_re, back_im = right_mult(resid_re, resid_im, table_re, conj_im)
    wave_re, wave_im = left_mult(table_re, conj_im, back_re.astype(jnp.bfloat16), back_im.astype(jnp.bfloat16))
    object_re = lax.optimization_barrier(jnp.sum(probe_fr * wave_re + probe_fi * wave_im, axis=0))
    object_im = lax.optimization_barrier(jnp.sum(probe_fr * wave_im - probe_fi * wave_re, axis=0))
    update_re = patch_re * wave_re + patch_im * wave_im
    update_im = patch_re * wave_im - patch_im * wave_re
    return (jnp.stack([object_re, object_im]), jnp.stack([update_re, update_im]))

def reference(object_field, probe, patterns, offsets, counts):
    table_re, table_im = tables(PAT)
    flat_counts = counts.reshape(-1)
    zero_index = jnp.int32(0)

    def visit(number, carried):
        totals, probe_total = carried
        device = number // POS_DEV
        alive = number % POS_DEV < flat_counts[device]

        def work(inner):
            grad_total, probe_sum_now = inner
            start_row = offsets[0, number].astype(jnp.int32)
            start_col = offsets[1, number].astype(jnp.int32)
            patch = lax.dynamic_slice(object_field, (zero_index, start_row, start_col), (2, PAT, PAT))
            object_term, probe_term = position(patch[0], patch[1], patterns[number], probe[0], probe[1], table_re, table_im)
            previous = lax.dynamic_slice(grad_total, (zero_index, start_row, start_col), (2, PAT, PAT))
            grad_total = lax.dynamic_update_slice(grad_total, previous + object_term, (zero_index, start_row, start_col))
            return (grad_total, probe_sum_now + probe_term)
        return lax.cond(alive, work, lambda inner: inner, (totals, probe_total))
    start = (jnp.zeros(object_field.shape, jnp.float32), jnp.zeros((2, MODES, PAT, PAT), jnp.float32))
    object_grad, probe_grad = lax.fori_loop(0, NPOS, visit, start)
    return (object_grad, probe_grad)
```

```python
import math

import jax
import jax.numpy as jnp
import numpy as np
from jax import lax
from jax.experimental import pallas as pl
from jax.experimental.pallas import tpu as pltpu
from jax.sharding import Mesh, PartitionSpec as P

LANES = 128
CHUNK = 32


def tables(length):
    index = np.arange(length)
    angle = (index[:, None] * index[None, :] % length) * (2.0 * math.pi / length)
    factor = 1.0 / math.sqrt(length)
    table_re = (np.cos(angle) * factor).astype(jnp.bfloat16)
    table_im = (-np.sin(angle) * factor).astype(jnp.bfloat16)
    forward = np.block([[table_re, table_im], [-table_im, table_re]])
    backward = np.block([[table_re, -table_im], [table_im, table_re]])
    return (forward.astype(jnp.bfloat16), backward.astype(jnp.bfloat16))


def slots_kernel(
    meta, tile, above, below, left, right, corner_left, corner_right, patterns, probe_hbm,
    forward_hbm, backward_hbm,
    center_out, top_out, bottom_out, left_out, right_out, keep_out, send_out,
    ext, totals, pat, probe, forward, backward, probe_total, obj, psi, half, field, wave, sems,
):
    slots, width = pat.shape[0], pat.shape[1]
    modes = probe.shape[1]
    tile_rows = tile.shape[1]
    blocks = tile.shape[2] // LANES
    last = blocks + 1
    margin = above.shape[1]
    low_end = margin + tile_rows
    moves = []

    def begin(source, target):
        move = pltpu.make_async_copy(source, target, sems.at[len(moves)])
        move.start()
        moves.append(move)

    for j in range(blocks):
        span = pl.ds(j * LANES, LANES)
        begin(tile.at[:, :, span], ext.at[:, 1 + j, pl.ds(margin, tile_rows), :])
        begin(above.at[:, :, span], ext.at[:, 1 + j, pl.ds(0, margin), :])
        begin(below.at[:, :, span], ext.at[:, 1 + j, pl.ds(low_end, margin), :])
    for side, corner, j in ((left, corner_left, 0), (right, corner_right, last)):
        begin(side, ext.at[:, j, pl.ds(margin, tile_rows), :])
        begin(corner.at[:, pl.ds(0, margin), :], ext.at[:, j, pl.ds(0, margin), :])
        begin(corner.at[:, pl.ds(margin, margin), :], ext.at[:, j, pl.ds(low_end, margin), :])
    begin(probe_hbm, probe)
    begin(forward_hbm, forward)
    begin(backward_hbm, backward)
    begin(patterns, pat)
    totals[...] = jnp.zeros_like(totals)
    probe_total[...] = jnp.zeros_like(probe_total)
    for move in moves:
        move.wait()

    lane = lax.broadcasted_iota(jnp.int32, (CHUNK, LANES), 1)

    def visit(number, carry):
        row = meta[number]
        col = meta[slots + number]
        block = jnp.minimum(col // LANES, blocks - 1)
        rest = col - block * LANES
        back_shift = lax.rem(LANES - rest, LANES)
        shift = lax.rem(rest, LANES)
        from_first = lane < LANES - rest
        at_or_after = lane >= rest

        for c in range(width // CHUNK):
            rows = pl.ds(c * CHUNK, CHUNK)
            source = pl.ds(row + c * CHUNK, CHUNK)
            patch = []
            for p in range(2):
                parts = [
                    pltpu.roll(ext[p, block + j, source, :], back_shift, 1) for j in range(3)
                ]
                whole = jnp.concatenate(
                    [
                        jnp.where(from_first, parts[0], parts[1]),
                        jnp.where(from_first, parts[1], parts[2]),
                    ],
                    axis=1,
                )
                obj[p, rows, :] = whole
                patch.append(whole)
            for k in range(modes):
                probe_re = probe[0, k, rows, :].astype(jnp.float32)
                probe_im = probe[1, k, rows, :].astype(jnp.float32)
                exit_re = probe_re * patch[0] - probe_im * patch[1]
                exit_im = probe_re * patch[1] + probe_im * patch[0]
                psi[k, rows, pl.ds(0, width)] = exit_re.astype(jnp.bfloat16)
                psi[k, rows, pl.ds(width, width)] = exit_im.astype(jnp.bfloat16)

        for k in range(modes):
            product = jnp.dot(psi[k], forward[...], preferred_element_type=jnp.float32)
            half[k, pl.ds(0, width), :] = product[:, :width].astype(jnp.bfloat16)
            half[k, pl.ds(width, width), :] = product[:, width:].astype(jnp.bfloat16)
        for k in range(modes):
            field[k] = jnp.dot(backward[...], half[k], preferred_element_type=jnp.float32)

        for c in range(width // CHUNK):
            rows = pl.ds(c * CHUNK, CHUNK)
            rows_im = pl.ds(width + c * CHUNK, CHUNK)
            values = [(field[k, rows, :], field[k, rows_im, :]) for k in range(modes)]
            intensity = sum(re * re + im * im for re, im in values)
            ratio = 1.0 - pat[number, rows, :] * lax.rsqrt(jnp.maximum(intensity, 1.0))
            for k, (re, im) in enumerate(values):
                psi[k, rows, pl.ds(0, width)] = (re * ratio).astype(jnp.bfloat16)
                psi[k, rows, pl.ds(width, width)] = (im * ratio).astype(jnp.bfloat16)

        for k in range(modes):
            product = jnp.dot(psi[k], backward[...], preferred_element_type=jnp.float32)
            half[k, pl.ds(0, width), :] = product[:, :width].astype(jnp.bfloat16)
            half[k, pl.ds(width, width), :] = product[:, width:].astype(jnp.bfloat16)
        for k in range(modes):
            wave[k] = jnp.dot(forward[...], half[k], preferred_element_type=jnp.float32)

        for c in range(width // CHUNK):
            rows = pl.ds(c * CHUNK, CHUNK)
            rows_im = pl.ds(width + c * CHUNK, CHUNK)
            target = pl.ds(row + c * CHUNK, CHUNK)
            patch_re = obj[0, rows, :]
            patch_im = obj[1, rows, :]
            term = [jnp.zeros((CHUNK, width), jnp.float32)] * 2
            for k in range(modes):
                probe_re = probe[0, k, rows, :].astype(jnp.float32)
                probe_im = probe[1, k, rows, :].astype(jnp.float32)
                wave_re = wave[k, rows, :]
                wave_im = wave[k, rows_im, :]
                term[0] = term[0] + (probe_re * wave_re + probe_im * wave_im)
                term[1] = term[1] + (probe_re * wave_im - probe_im * wave_re)
                probe_total[0, k, rows, :] += patch_re * wave_re + patch_im * wave_im
                probe_total[1, k, rows, :] += patch_re * wave_im - patch_im * wave_re
            for p in range(2):
                first = pltpu.roll(term[p][:, :LANES], shift, 1)
                second = pltpu.roll(term[p][:, LANES:], shift, 1)
                totals[p, block, target, :] += jnp.where(at_or_after, first, 0.0)
                totals[p, block + 1, target, :] += jnp.where(at_or_after, second, first)
                totals[p, block + 2, target, :] += jnp.where(at_or_after, 0.0, second)
        return carry

    lax.fori_loop(0, meta[2 * slots], visit, 0)

    core = meta[2 * slots + 1]
    moves.clear()
    begin(probe_total.at[1 - core], send_out)
    begin(totals.at[:, 0], left_out)
    begin(totals.at[:, last], right_out)
    begin(probe_total.at[core], keep_out)
    for j in range(blocks):
        span = pl.ds(j * LANES, LANES)
        begin(totals.at[:, 1 + j, pl.ds(0, margin), :], top_out.at[:, :, span])
        begin(totals.at[:, 1 + j, pl.ds(low_end, margin), :], bottom_out.at[:, :, span])
        begin(totals.at[:, 1 + j, pl.ds(margin, tile_rows), :], center_out.at[:, :, span])
    for move in moves:
        move.wait()


def run_slots(meta, tile, sides, patterns, probe, forward, backward):
    slots, width = patterns.shape[0], patterns.shape[1]
    modes = probe.shape[1]
    rows, cols = tile.shape[1], tile.shape[2]
    margin = width // 2
    blocks = cols // LANES
    f32 = jnp.float32
    bf16 = jnp.bfloat16
    out_shapes = [
        (2, rows, cols),
        (2, margin, cols),
        (2, margin, cols),
        (2, rows + 2 * margin, margin),
        (2, rows + 2 * margin, margin),
        (modes, width, width),
        (modes, width, width),
    ]
    hbm = pl.BlockSpec(memory_space=pl.ANY)
    work = slots * modes * width * width * width * 4 * 4 * 2
    return pl.pallas_call(
        slots_kernel,
        out_shape=[jax.ShapeDtypeStruct(shape, f32) for shape in out_shapes],
        in_specs=[pl.BlockSpec(memory_space=pltpu.SMEM)] + [hbm] * 11,
        out_specs=[hbm] * 7,
        scratch_shapes=[
            pltpu.VMEM((2, blocks + 2, rows + 2 * margin, LANES), f32),
            pltpu.VMEM((2, blocks + 2, rows + 2 * margin, LANES), f32),
            pltpu.VMEM(patterns.shape, f32),
            pltpu.VMEM(probe.shape, bf16),
            pltpu.VMEM(forward.shape, bf16),
            pltpu.VMEM(backward.shape, bf16),
            pltpu.VMEM((2, modes, width, width), f32),
            pltpu.VMEM((2, width, width), f32),
            pltpu.VMEM((modes, width, 2 * width), bf16),
            pltpu.VMEM((modes, 2 * width, width), bf16),
            pltpu.VMEM((modes, 2 * width, width), f32),
            pltpu.VMEM((modes, 2 * width, width), f32),
            pltpu.SemaphoreType.DMA((32,)),
        ],
        compiler_params=pltpu.CompilerParams(vmem_limit_bytes=48 * 1024 * 1024),
        cost_estimate=pl.CostEstimate(
            flops=work, bytes_accessed=20_000_000, transcendentals=slots * width * width
        ),
        name="slots",
    )(meta, tile, *sides, patterns, probe, forward, backward)


def up(block, axes):
    count = lax.axis_size(axes)
    return lax.ppermute(block, axes, [(i, i + 1) for i in range(count - 1)])


def down(block, axes):
    count = lax.axis_size(axes)
    return lax.ppermute(block, axes, [(i + 1, i) for i in range(count - 1)])


def on_device(row_axes, col_axes, core_axis, object_field, probe, patterns, offsets, counts):
    tile_rows, tile_cols = object_field.shape[1:]
    width = patterns.shape[1]
    modes = probe.shape[1]
    margin = width // 2
    chip_axes = row_axes + tuple(name for name in col_axes if name != core_axis)

    from_above = up(object_field[:, tile_rows - margin :, :], row_axes)
    from_below = down(object_field[:, :margin, :], row_axes)
    from_left = up(object_field[:, :, tile_cols - margin :], col_axes)
    from_right = down(object_field[:, :, :margin], col_axes)
    ends = jnp.concatenate([from_above, from_below], axis=1)
    corner_left = up(ends[:, :, tile_cols - margin :], col_axes)
    corner_right = down(ends[:, :, :margin], col_axes)

    base_row = lax.axis_index(row_axes) * tile_rows - margin
    base_col = lax.axis_index(col_axes) * tile_cols - margin
    core = lax.axis_index(core_axis)
    meta = jnp.concatenate(
        [offsets[0] - base_row, offsets[1] - base_col, counts[0], core.reshape(1)]
    ).astype(jnp.int32)
    forward, backward = tables(width)
    sides = (from_above, from_below, from_left, from_right, corner_left, corner_right)
    center, top, bottom, left, right, keep, send = run_slots(
        meta, object_field, sides, patterns, probe, jnp.asarray(forward), jnp.asarray(backward)
    )

    mates = [(0, 1), (1, 0)]
    received = lax.ppermute(send, core_axis, mates)
    to_left = up(right, col_axes)
    to_right = down(left, col_axes)
    pair = keep + received
    chips = lax.axis_size(chip_axes)
    pieces = pair.reshape(chips, modes * width // chips, width)
    pieces = lax.all_to_all(pieces, chip_axes, 0, 0, tiled=True)

    def spread(band, start):
        band = band.at[:, :, :margin].add(to_left[:, start : start + margin])
        return band.at[:, :, tile_cols - margin :].add(to_right[:, start : start + margin])

    top = spread(top, 0)
    bottom = spread(bottom, margin + tile_rows)
    add_top = up(bottom, row_axes)
    add_bottom = down(top, row_axes)

    mine = jnp.sum(pieces, axis=0)
    gathered = lax.all_to_all(
        jnp.broadcast_to(mine, pieces.shape), chip_axes, 0, 0, tiled=True
    ).reshape(modes, width, width)
    other = lax.ppermute(gathered, core_axis, mates)
    probe_grad = jnp.where(
        core == 0, jnp.stack([gathered, other]), jnp.stack([other, gathered])
    )

    center = center.at[:, :, :margin].add(to_left[:, margin : margin + tile_rows])
    center = center.at[:, :, tile_cols - margin :].add(to_right[:, margin : margin + tile_rows])
    center = center.at[:, :margin, :].add(add_top)
    center = center.at[:, tile_rows - margin :, :].add(add_bottom)
    return (center, probe_grad)


def solution(mesh):
    rows, cols = mesh.devices.shape
    side = math.isqrt(rows)
    fine = Mesh(mesh.devices.reshape(side, side, cols // 2, 2), ("x", "y", "z", "core"))
    row_axes, col_axes = ("x", "y"), ("z", "core")
    every = row_axes + col_axes
    in_specs = (
        P(None, row_axes, col_axes),
        P(),
        P(every, None, None),
        P(None, every),
        P(row_axes, col_axes),
    )
    out_specs = (P(None, row_axes, col_axes), P())

    def body(*args):
        return on_device(row_axes, col_axes, "core", *args)

    return jax.shard_map(
        body, mesh=fine, in_specs=in_specs, out_specs=out_specs, check_vma=False
    )
```

```python
import math

import jax
import jax.numpy as jnp
import numpy as np
from jax import lax
from jax.experimental import pallas as pl
from jax.experimental.pallas import tpu as pltpu
from jax.sharding import Mesh, PartitionSpec as P

LANES = 128
CHUNK = 32
F32 = jnp.float32
BF16 = jnp.bfloat16
RIGHT = (0, 2)
LEFT = (1, 3)
MIB = 1024 * 1024
FREE = pl.BlockSpec(memory_space=pl.ANY)
VMEM = pl.BlockSpec(memory_space=pltpu.VMEM)
ROW, COL, CORE = ("x", "y"), ("z", "core"), "core"
CHIP = ("x", "y", "z")
SMEM = pl.BlockSpec(memory_space=pltpu.SMEM)


def tables(length):
    index = np.arange(length // 2)
    parts = []
    for parity in range(2):
        product = index[:, None] * (2 * index[None, :] + parity) % length
        angle = product * (2.0 * math.pi / length)
        factor = 1.0 / math.sqrt(length)
        re = (np.cos(angle) * factor).astype(BF16)
        im = (-np.sin(angle) * factor).astype(BF16)
        right = np.block([[re, im], [-im, re]])
        parts += [right, right.T]
    return np.stack(parts).astype(BF16)


def dot(a, b):
    return jnp.dot(a, b, preferred_element_type=F32)


def one_slot(number, row, col, ext, pat, probe, table, totals, keep, send, work):
    obj, term, psi, half, field, ratio = work
    width = pat.shape[1]
    modes = probe.shape[1]
    mid = width // 2
    blocks = ext.shape[1] - 2
    core = lax.axis_index(CORE)
    block = jnp.minimum(col // LANES, blocks - 1)
    rest = col - block * LANES
    back_shift = lax.rem(LANES - rest, LANES)
    shift = lax.rem(rest, LANES)
    lane = lax.broadcasted_iota(jnp.int32, (CHUNK, LANES), 1)
    from_first = lane < LANES - rest
    at_or_after = lane >= rest
    turn = (core + jnp.zeros((CHUNK, LANES), jnp.int32)) == 0
    low, high = pl.ds(0, mid), pl.ds(mid, mid)

    def span(c, base=0):
        return pl.ds(base + c * CHUNK, CHUNK)

    def gather_patch():
        for c in range(width // CHUNK):
            source = pl.ds(row + c * CHUNK, CHUNK)
            patch = []
            for p in range(2):
                parts = [
                    pltpu.roll(ext[p, block + j, source, :], back_shift, 1) for j in range(3)
                ]
                patch.append(
                    [
                        jnp.where(from_first, parts[0], parts[1]),
                        jnp.where(from_first, parts[1], parts[2]),
                    ]
                )
            for side, lanes in enumerate((low, high)):
                re, im = patch[0][side], patch[1][side]
                obj[0, span(c), lanes] = re
                obj[1, span(c), lanes] = im

    def make_psi(k):
        for c in range(width // CHUNK):
            waves = []
            for lanes in (low, high):
                o_re, o_im = obj[0, span(c), lanes], obj[1, span(c), lanes]
                p_re = probe[0, k, span(c), lanes]
                p_im = probe[1, k, span(c), lanes]
                waves.append((p_re * o_re - p_im * o_im, p_re * o_im + p_im * o_re))
            for part, lanes in enumerate((low, high)):
                a, b = waves[0][part], waves[1][part]
                psi[k, 0, span(c), lanes] = (a + b).astype(BF16)
                psi[k, 1, span(c), lanes] = (a - b).astype(BF16)

    def right_forward(k):
        for parity, lanes in enumerate((low, high)):
            y = dot(psi[k, parity], table[RIGHT[parity]])
            top, bottom = y[:mid], y[mid:]
            total, difference = (top + bottom).astype(BF16), (top - bottom).astype(BF16)
            half[k, 0, low, lanes] = total[:, :mid]
            half[k, 0, high, lanes] = total[:, mid:]
            half[k, 1, low, lanes] = difference[:, :mid]
            half[k, 1, high, lanes] = difference[:, mid:]

    def left_forward(k):
        for parity in range(2):
            field[k, parity] = dot(table[LEFT[parity]], half[k, parity])

    def make_ratio():
        for parity in range(2):
            for c in range(mid // CHUNK):
                total = None
                for k in range(modes):
                    re, im = field[k, parity, span(c), :], field[k, parity, span(c, mid), :]
                    square = re * re + im * im
                    total = square if total is None else total + square
                measured = pat[number, span(c, parity * mid), :]
                ratio[parity, span(c), :] = 1.0 - measured * lax.rsqrt(jnp.maximum(total, 1.0))

    def make_chi(k):
        for parity in range(2):
            for c in range(mid // CHUNK):
                scale = ratio[parity, span(c), :]
                re = (field[k, parity, span(c), :] * scale).astype(BF16)
                im = (field[k, parity, span(c, mid), :] * scale).astype(BF16)
                rows = span(c, parity * mid)
                psi[k, 0, rows, low] = re[:, :mid]
                psi[k, 0, rows, high] = im[:, :mid]
                psi[k, 1, rows, low] = re[:, mid:]
                psi[k, 1, rows, high] = im[:, mid:]

    def right_backward(k):
        even = dot(psi[k, 0], table[LEFT[0]])
        odd = dot(psi[k, 1], table[LEFT[1]])
        for value, lanes in (((even + odd).astype(BF16), low), ((even - odd).astype(BF16), high)):
            for parity in range(2):
                rows = value[parity * mid : parity * mid + mid]
                half[k, parity, low, lanes] = rows[:, :mid]
                half[k, parity, high, lanes] = rows[:, mid:]

    def left_backward(k):
        for parity in range(2):
            field[k, parity] = dot(table[RIGHT[parity]], half[k, parity])

    def collect(k):
        for c in range(mid // CHUNK):
            even_re, odd_re = field[k, 0, span(c), :], field[k, 1, span(c), :]
            even_im, odd_im = field[k, 0, span(c, mid), :], field[k, 1, span(c, mid), :]
            for rows, re, im in (
                (span(c), even_re + odd_re, even_im + odd_im),
                (span(c, mid), even_re - odd_re, even_im - odd_im),
            ):
                p_re, p_im = probe[0, k, rows, :], probe[1, k, rows, :]
                add_re = p_re * re + p_im * im
                add_im = p_re * im - p_im * re
                if k == 0:
                    term[0, rows, :] = add_re
                    term[1, rows, :] = add_im
                else:
                    term[0, rows, :] += add_re
                    term[1, rows, :] += add_im
                o_re, o_im = obj[0, rows, :], obj[1, rows, :]
                keep[k, rows, :] += o_re * re + o_im * im
                send[k, rows, :] += o_re * im - o_im * re

    def turn_patch():
        for c in range(width // CHUNK):
            for lanes in (low, high):
                re, im = obj[0, span(c), lanes], obj[1, span(c), lanes]
                obj[0, span(c), lanes] = jnp.where(turn, re, -im)
                obj[1, span(c), lanes] = jnp.where(turn, im, re)

    def add_term():
        for c in range(width // CHUNK):
            target = pl.ds(row + c * CHUNK, CHUNK)
            for p in range(2):
                first = pltpu.roll(term[p, span(c), low], shift, 1)
                second = pltpu.roll(term[p, span(c), high], shift, 1)
                totals[p, block, target, :] += jnp.where(at_or_after, first, 0.0)
                totals[p, block + 1, target, :] += jnp.where(at_or_after, second, first)
                totals[p, block + 2, target, :] += jnp.where(at_or_after, 0.0, second)

    gather_patch()
    make_psi(0)
    make_psi(1)
    for k in range(modes):
        right_forward(k)
        if k + 2 < modes:
            make_psi(k + 2)
        if k == modes - 2:
            turn_patch()
        if k >= 1:
            left_forward(k - 1)
    left_forward(modes - 1)
    make_ratio()
    make_chi(0)
    make_chi(1)
    for k in range(modes):
        right_backward(k)
        if k + 2 < modes:
            make_chi(k + 2)
        if k >= 1:
            left_backward(k - 1)
        if k >= 2:
            collect(k - 2)
    left_backward(modes - 1)
    collect(modes - 2)
    collect(modes - 1)
    add_term()


class Moves:
    def __init__(self, sems):
        self.sems = sems
        self.started = []

    def begin(self, source, target):
        move = pltpu.make_async_copy(source, target, self.sems.at[len(self.started)])
        move.start()
        self.started.append(move)

    def wait(self):
        for move in self.started:
            move.wait()


def visit_all(later, offsets, counts, tile_rows, tile_cols, ext, pat, *rest):
    width = pat.shape[1]
    margin = width // 2
    base_row = lax.axis_index(ROW) * tile_rows - margin
    base_col = lax.axis_index(COL) * tile_cols - margin

    def visit(number, carry):
        row = offsets[0, number] - base_row
        col = offsets[1, number] - base_col
        beyond = jnp.logical_or(row < margin, row + width > margin + tile_rows)

        @pl.when(beyond if later else jnp.logical_not(beyond))
        def _():
            one_slot(number, row, col, ext, pat, *rest)

        return carry

    lax.fori_loop(0, counts[0, 0], visit, 0)


def first_kernel(
    offsets, counts, tile, inner, outer, pat, probe, table,
    ext, totals, keep, send, obj, term, psi, half, field, ratio, sems,
):
    rows, cols = tile.shape[1:]
    margin = inner.shape[2]
    last = cols // LANES + 1
    core = lax.axis_index(CORE)
    middle = pl.ds(margin, rows)
    moves = Moves(sems)
    for j in range(1, last):
        moves.begin(tile.at[:, :, pl.ds((j - 1) * LANES, LANES)], ext.at[:, j, middle, :])
    moves.begin(inner, ext.at[:, (1 - core) * last, middle, :])
    moves.begin(outer, ext.at[:, core * last, middle, :])
    totals[...] = jnp.zeros_like(totals)
    keep[...] = jnp.zeros_like(keep)
    send[...] = jnp.zeros_like(send)
    moves.wait()
    work = (obj, term, psi, half, field, ratio)
    visit_all(False, offsets, counts, rows, cols, ext, pat, probe, table, totals, keep, send, work)


def second_kernel(
    offsets, counts, above, below, corner_above, corner_below, ext_in, totals_in, keep_in,
    send_in, pat, probe, table,
    totals, keep, send, inner_out, outer_out, inner_ends, outer_ends,
    ext, obj, term, psi, half, field, ratio, sems,
):
    margin, cols = above.shape[1:]
    last = ext.shape[1] - 1
    rows = ext.shape[2] - 2 * margin
    core = lax.axis_index(CORE)
    inner_block, outer_block = (1 - core) * last, core * last
    top, middle, bottom = pl.ds(0, margin), pl.ds(margin, rows), pl.ds(margin + rows, margin)
    moves = Moves(sems)
    moves.begin(ext_in.at[:, :, middle, :], ext.at[:, :, middle, :])
    for j in range(1, last):
        lanes = pl.ds((j - 1) * LANES, LANES)
        moves.begin(above.at[:, :, lanes], ext.at[:, j, top, :])
        moves.begin(below.at[:, :, lanes], ext.at[:, j, bottom, :])
    for n, j in enumerate((inner_block, outer_block)):
        lanes = pl.ds(n * margin, margin)
        moves.begin(corner_above.at[:, :, lanes], ext.at[:, j, top, :])
        moves.begin(corner_below.at[:, :, lanes], ext.at[:, j, bottom, :])
    totals[...] = totals_in[...]
    keep[...] = keep_in[...]
    send[...] = send_in[...]
    moves.wait()
    work = (obj, term, psi, half, field, ratio)
    visit_all(True, offsets, counts, rows, cols, ext, pat, probe, table, totals, keep, send, work)
    moves = Moves(sems)
    for edge, ends, j in (
        (outer_out, outer_ends, outer_block), (inner_out, inner_ends, inner_block)
    ):
        moves.begin(totals.at[:, j, top, :], ends.at[:, pl.ds(0, margin), :])
        moves.begin(totals.at[:, j, bottom, :], ends.at[:, pl.ds(margin, margin), :])
        moves.begin(totals.at[:, j, middle, :], edge)
    moves.wait()


def slot_scratch(modes, width):
    return [
        pltpu.VMEM((2, width, width), F32),
        pltpu.VMEM((2, width, width), F32),
        pltpu.VMEM((modes, 2, width, width), BF16),
        pltpu.VMEM((modes, 2, width, width), BF16),
        pltpu.VMEM((modes, 2, width, width), F32),
        pltpu.VMEM((2, width // 2, width), F32),
        pltpu.SemaphoreType.DMA((16,)),
    ]


def shapes(*dims):
    return [jax.ShapeDtypeStruct(shape, F32) for shape in dims]


def cost(slots, modes, width):
    return pl.CostEstimate(
        flops=slots * modes * width * width * width * 16,
        bytes_accessed=30 * MIB,
        transcendentals=slots * width * width,
    )


def first_slots(offsets, counts, tile, inner, outer, patterns, probe, table):
    modes, width = probe.shape[1:3]
    rows, cols = tile.shape[1:]
    grown = (2, cols // LANES + 2, rows + 2 * inner.shape[2], LANES)
    plane = (modes, width, width)
    return pl.pallas_call(
        first_kernel,
        out_shape=shapes(grown, grown, plane, plane),
        in_specs=[SMEM] * 2 + [FREE] * 3 + [VMEM] * 3,
        out_specs=[VMEM] * 4,
        scratch_shapes=slot_scratch(modes, width),
        compiler_params=pltpu.CompilerParams(vmem_limit_bytes=24 * MIB),
        cost_estimate=cost(4, modes, width),
        name="slots_first",
    )(offsets, counts, tile, inner, outer, patterns, probe, table)


def second_slots(offsets, counts, sides, ext, totals, keep, send, patterns, probe, table):
    modes, width = probe.shape[1:3]
    margin = sides[0].shape[1]
    rows = ext.shape[2] - 2 * margin
    edge, ends = (2, rows, margin), (2, 2 * margin, margin)
    return pl.pallas_call(
        second_kernel,
        out_shape=shapes(totals.shape, keep.shape, send.shape, edge, edge, ends, ends),
        in_specs=[SMEM] * 2 + [FREE] * 5 + [VMEM] * 6,
        out_specs=[VMEM] * 3 + [FREE] * 4,
        scratch_shapes=[pltpu.VMEM(ext.shape, F32)] + slot_scratch(modes, width),
        input_output_aliases={7: 0, 8: 1, 9: 2},
        compiler_params=pltpu.CompilerParams(vmem_limit_bytes=24 * MIB),
        cost_estimate=cost(4, modes, width),
        name="slots_second",
    )(offsets, counts, *sides, ext, totals, keep, send, patterns, probe, table)


def prepare_kernel(patterns, probe, out, wide, moving):
    wide[...] = probe[...].astype(F32)
    slots, width = patterns.shape[:2]
    mid = width // 2
    source = lax.broadcasted_iota(jnp.int32, (width, width), 0)
    target = lax.broadcasted_iota(jnp.int32, (width, width), 1)
    wanted = jnp.where(target < mid, 2 * target, 2 * target - (width - 1))
    pick = (source == wanted).astype(BF16)

    def one(number, carry):
        value = patterns[number]
        total = None
        for _ in range(3):
            part = value.astype(BF16)
            value = value - part.astype(F32)
            moved = dot(part, pick)
            total = moved if total is None else total + moved
        for side in range(2):
            lanes = pl.ds(side * mid, mid)
            moving[side] = total[:, side * mid : side * mid + mid]
            for parity in range(2):
                out[number, pl.ds(parity * mid, mid), lanes] = moving[side, pl.ds(parity, mid, 2), :]
        return carry

    lax.fori_loop(0, slots, one, 0)


def prepare(patterns, probe):
    return pl.pallas_call(
        prepare_kernel,
        out_shape=shapes(patterns.shape, probe.shape),
        in_specs=[VMEM] * 2,
        out_specs=[VMEM] * 2,
        scratch_shapes=[pltpu.VMEM((2, patterns.shape[1], patterns.shape[2] // 2), F32)],
        compiler_params=pltpu.CompilerParams(vmem_limit_bytes=12 * MIB),
        cost_estimate=pl.CostEstimate(
            flops=patterns.size * 256 * 6, bytes_accessed=9 * MIB, transcendentals=0
        ),
        name="prepare",
    )(patterns, probe)


def cut_kernel(tile, top, bottom, inner, outer, sems):
    margin = top.shape[1]
    rows, cols = tile.shape[1:]
    core = lax.axis_index(CORE)

    def strip(start):
        return tile.at[:, :, pl.ds(pl.multiple_of(start, LANES), margin)]

    moves = Moves(sems)
    moves.begin(tile.at[:, pl.ds(rows - margin, margin), :], bottom)
    moves.begin(tile.at[:, pl.ds(0, margin), :], top)
    moves.begin(strip(core * (cols - margin)), outer)
    moves.begin(strip((1 - core) * (cols - margin)), inner)
    moves.wait()


def cut(tile, margin):
    rows, cols = tile.shape[1:]
    return pl.pallas_call(
        cut_kernel,
        out_shape=shapes((2, margin, cols), (2, margin, cols), (2, rows, margin), (2, rows, margin)),
        in_specs=[FREE],
        out_specs=[FREE] * 4,
        scratch_shapes=[pltpu.SemaphoreType.DMA((4,))],
        compiler_params=pltpu.CompilerParams(vmem_limit_bytes=MIB),
        cost_estimate=pl.CostEstimate(flops=0, bytes_accessed=4 * MIB, transcendentals=0),
        name="cut",
    )(tile)


def add_sides(add, inner, outer, last):
    core = lax.axis_index(CORE)

    @pl.when(core == 0)
    def _():
        add(outer, 0)
        add(inner, last)

    @pl.when(core != 0)
    def _():
        add(inner, 0)
        add(outer, last)


def mix_kernel(totals, inner, outer, keep, received, top, bottom, pair):
    margin = top.shape[1]
    blocks = totals.shape[1] - 2
    low_end = totals.shape[2] - margin
    sign = jnp.where(lax.axis_index(CORE) == 0, -1.0, 1.0).astype(F32)
    for k in range(keep.shape[0]):
        pair[k] = keep[k] + received[k] * sign
    for j in range(blocks):
        lanes = pl.ds(j * LANES, LANES)
        top[:, :, lanes] = totals[:, 1 + j, :margin, :]
        bottom[:, :, lanes] = totals[:, 1 + j, low_end:, :]

    def add(side, j):
        lanes = pl.ds(j * LANES, LANES)
        top[:, :, lanes] += side[:, :margin, :]
        bottom[:, :, lanes] += side[:, margin:, :]

    add_sides(add, inner, outer, blocks - 1)


def mix(totals, inner, outer, keep, received):
    margin = inner.shape[1] // 2
    strip = (2, margin, (totals.shape[1] - 2) * LANES)
    return pl.pallas_call(
        mix_kernel,
        out_shape=shapes(strip, strip, keep.shape),
        in_specs=[VMEM] * 5,
        out_specs=[VMEM] * 3,
        compiler_params=pltpu.CompilerParams(vmem_limit_bytes=12 * MIB),
        cost_estimate=pl.CostEstimate(flops=600_000, bytes_accessed=6 * MIB, transcendentals=0),
        name="mix",
    )(totals, inner, outer, keep, received)


def fold_kernel(pieces, out):
    total = pieces[0]
    for n in range(1, pieces.shape[0]):
        total = total + pieces[n]
    for n in range(pieces.shape[0]):
        out[n] = total


def fold(pieces):
    return pl.pallas_call(
        fold_kernel,
        out_shape=jax.ShapeDtypeStruct(pieces.shape, F32),
        in_specs=[VMEM],
        out_specs=VMEM,
        compiler_params=pltpu.CompilerParams(vmem_limit_bytes=4 * MIB),
        cost_estimate=pl.CostEstimate(flops=300_000, bytes_accessed=2 * MIB, transcendentals=0),
        name="fold",
    )(pieces)


def finish_kernel(totals, inner, outer, above, below, out, result, sems):
    margin = above.shape[1]
    rows = inner.shape[1]
    blocks = totals.shape[1] - 2
    moves = Moves(sems)
    for p in range(2):
        for j in range(blocks):
            lanes = pl.ds(j * LANES, LANES)
            result[p, :, lanes] = totals[p, 1 + j, margin : margin + rows, :]
        result[p, :margin, :] += above[p]
        result[p, rows - margin :, :] += below[p]

        def add(side, j):
            result[p, :, pl.ds(j * LANES, LANES)] += side[p]

        add_sides(add, inner, outer, blocks - 1)
        moves.begin(result.at[p], out.at[p])
    moves.wait()


def finish(totals, inner, outer, above, below):
    shape = (2, inner.shape[1], above.shape[2])
    return pl.pallas_call(
        finish_kernel,
        out_shape=jax.ShapeDtypeStruct(shape, F32),
        in_specs=[VMEM] * 5,
        out_specs=FREE,
        scratch_shapes=[pltpu.VMEM(shape, F32), pltpu.SemaphoreType.DMA((2,))],
        compiler_params=pltpu.CompilerParams(vmem_limit_bytes=14 * MIB),
        cost_estimate=pl.CostEstimate(flops=600_000, bytes_accessed=7 * MIB, transcendentals=0),
        name="finish",
    )(totals, inner, outer, above, below)


def join_kernel(own, other, out, sems):
    core = lax.axis_index(CORE)
    moves = Moves(sems)
    moves.begin(own, out.at[core])
    moves.begin(other, out.at[1 - core])
    moves.wait()


def join(own, other):
    return pl.pallas_call(
        join_kernel,
        out_shape=jax.ShapeDtypeStruct((2,) + own.shape, F32),
        in_specs=[FREE, FREE],
        out_specs=FREE,
        scratch_shapes=[pltpu.SemaphoreType.DMA((2,))],
        compiler_params=pltpu.CompilerParams(vmem_limit_bytes=MIB),
        cost_estimate=pl.CostEstimate(flops=0, bytes_accessed=4 * MIB, transcendentals=0),
        name="join",
    )(own, other)


def up(block, axes):
    count = lax.axis_size(axes)
    return lax.ppermute(block, axes, [(i, i + 1) for i in range(count - 1)])


def down(block, axes):
    count = lax.axis_size(axes)
    return lax.ppermute(block, axes, [(i + 1, i) for i in range(count - 1)])


def swap_inner(block, axes):
    count = lax.axis_size(axes)
    return lax.ppermute(block, axes, [(i, i ^ 1) for i in range(count)])


def swap_outer(block, axes):
    count = lax.axis_size(axes)
    pairs = [(i, i + 1) for i in range(1, count - 1, 2)]
    return lax.ppermute(block, axes, pairs + [(j, i) for i, j in pairs])


def on_device(object_field, probe, patterns, offsets, counts):
    rows = object_field.shape[1]
    width = patterns.shape[1]
    modes = probe.shape[1]
    margin = width // 2

    top, bottom, inner, outer = cut(object_field, margin)
    from_above = up(bottom, ROW)
    from_below = down(top, ROW)
    outer = swap_outer(outer, COL)
    inner = swap_inner(inner, COL)

    def corners(start):
        span = slice(start, start + margin)
        return jnp.concatenate([inner[:, span], outer[:, span]], axis=2)

    corner_above = up(corners(rows - margin), ROW)
    corner_below = down(corners(0), ROW)

    table = jnp.asarray(tables(width))
    measured, wide = prepare(patterns, probe)
    ext, totals, keep, send = first_slots(
        offsets, counts, object_field, inner, outer, measured, wide, table
    )
    sides = (from_above, from_below, corner_above, corner_below)
    totals, keep, send, inner, outer, inner_ends, outer_ends = second_slots(
        offsets, counts, sides, ext, totals, keep, send, measured, wide, table
    )

    outer_ends = swap_outer(outer_ends, COL)
    inner_ends = swap_inner(inner_ends, COL)
    received = swap_inner(send, COL)
    top, bottom, pair = mix(totals, inner_ends, outer_ends, keep, received)
    chips = lax.axis_size(CHIP)
    pieces = pair.reshape(chips, modes * width // chips, width)
    pieces = lax.all_to_all(pieces, CHIP, 0, 0, tiled=True)
    from_above = up(bottom, ROW)
    from_below = down(top, ROW)
    outer = swap_outer(outer, COL)
    inner = swap_inner(inner, COL)
    pieces, from_above, from_below = lax.optimization_barrier((pieces, from_above, from_below))
    gathered = lax.all_to_all(fold(pieces), CHIP, 0, 0, tiled=True).reshape(modes, width, width)
    object_grad = finish(totals, inner, outer, from_above, from_below)
    gathered, object_grad = lax.optimization_barrier((gathered, object_grad))
    other = swap_inner(gathered, COL)
    return (object_grad, join(gathered, other))


def solution(mesh):
    rows, cols = mesh.devices.shape
    side = math.isqrt(rows)
    fine = Mesh(mesh.devices.reshape(side, side, cols // 2, 2), CHIP + (CORE,))
    in_specs = (P(None, ROW, COL), P(), P(ROW + COL, None, None), P(None, ROW + COL), P(ROW, COL))
    out_specs = (P(None, ROW, COL), P())
    return jax.shard_map(
        on_device, mesh=fine, in_specs=in_specs, out_specs=out_specs, check_vma=False
    )
```

```python
import math

import jax
import jax.numpy as jnp
import numpy as np
from jax import lax
from jax.experimental import pallas as pl
from jax.experimental.pallas import tpu as pltpu
from jax.sharding import Mesh, PartitionSpec as P

LANES = 128
CHUNK = 32
F32 = jnp.float32
BF16 = jnp.bfloat16
RIGHT = (0, 2)
LEFT = (1, 3)
MIB = 1024 * 1024
SPARE = 15
FREE = pl.BlockSpec(memory_space=pl.ANY)
VMEM = pl.BlockSpec(memory_space=pltpu.VMEM)
ROW, COL, CORE = ("x", "y"), ("z", "core"), "core"
CHIP = ("x", "y", "z")
SMEM = pl.BlockSpec(memory_space=pltpu.SMEM)


def tables(length):
    index = np.arange(length // 2)
    parts = []
    for parity in range(2):
        product = index[:, None] * (2 * index[None, :] + parity) % length
        angle = product * (2.0 * math.pi / length)
        factor = 1.0 / math.sqrt(length)
        re = (np.cos(angle) * factor).astype(BF16)
        im = (-np.sin(angle) * factor).astype(BF16)
        right = np.block([[re, im], [-im, re]])
        parts += [right, right.T]
    return np.stack(parts).astype(BF16)


def dot(a, b):
    return jnp.dot(a, b, preferred_element_type=F32)


def one_slot(number, row, col, ext, pat, probe, table, totals, keep, send, work):
    obj, term, psi, half, field, ratio = work
    width = pat.shape[1]
    modes = probe.shape[1]
    mid = width // 2
    blocks = ext.shape[1] - 2
    core = lax.axis_index(CORE)
    block = jnp.minimum(col // LANES, blocks - 1)
    rest = col - block * LANES
    back_shift = lax.rem(LANES - rest, LANES)
    shift = lax.rem(rest, LANES)
    lane = lax.broadcasted_iota(jnp.int32, (CHUNK, LANES), 1)
    from_first = lane < LANES - rest
    at_or_after = lane >= rest
    turn = (core + jnp.zeros((CHUNK, LANES), jnp.int32)) == 0
    low, high = pl.ds(0, mid), pl.ds(mid, mid)

    def span(c, base=0):
        return pl.ds(base + c * CHUNK, CHUNK)

    def gather_patch():
        for c in range(width // CHUNK):
            source = pl.ds(row + c * CHUNK, CHUNK)
            patch = []
            for p in range(2):
                parts = [
                    pltpu.roll(ext[p, block + j, source, :], back_shift, 1) for j in range(3)
                ]
                patch.append(
                    [
                        jnp.where(from_first, parts[0], parts[1]),
                        jnp.where(from_first, parts[1], parts[2]),
                    ]
                )
            for side, lanes in enumerate((low, high)):
                re, im = patch[0][side], patch[1][side]
                obj[0, span(c), lanes] = re
                obj[1, span(c), lanes] = im

    def make_psi(k):
        for c in range(width // CHUNK):
            waves = []
            for lanes in (low, high):
                o_re, o_im = obj[0, span(c), lanes], obj[1, span(c), lanes]
                p_re = probe[0, k, span(c), lanes]
                p_im = probe[1, k, span(c), lanes]
                waves.append((p_re * o_re - p_im * o_im, p_re * o_im + p_im * o_re))
            for part, lanes in enumerate((low, high)):
                a, b = waves[0][part], waves[1][part]
                psi[k, 0, span(c), lanes] = (a + b).astype(BF16)
                psi[k, 1, span(c), lanes] = (a - b).astype(BF16)

    def right_forward(k):
        for parity, lanes in enumerate((low, high)):
            y = dot(psi[k, parity], table[RIGHT[parity]])
            top, bottom = y[:mid], y[mid:]
            total, difference = (top + bottom).astype(BF16), (top - bottom).astype(BF16)
            half[k, 0, low, lanes] = total[:, :mid]
            half[k, 0, high, lanes] = total[:, mid:]
            half[k, 1, low, lanes] = difference[:, :mid]
            half[k, 1, high, lanes] = difference[:, mid:]

    def left_forward(k):
        for parity in range(2):
            field[k, parity] = dot(table[LEFT[parity]], half[k, parity])

    def make_ratio():
        for parity in range(2):
            for c in range(mid // CHUNK):
                total = None
                for k in range(modes):
                    re, im = field[k, parity, span(c), :], field[k, parity, span(c, mid), :]
                    square = re * re + im * im
                    total = square if total is None else total + square
                measured = pat[number, span(c, parity * mid), :]
                ratio[parity, span(c), :] = 1.0 - measured * lax.rsqrt(jnp.maximum(total, 1.0))

    def make_chi(k):
        for parity in range(2):
            for c in range(mid // CHUNK):
                scale = ratio[parity, span(c), :]
                re = (field[k, parity, span(c), :] * scale).astype(BF16)
                im = (field[k, parity, span(c, mid), :] * scale).astype(BF16)
                rows = span(c, parity * mid)
                psi[k, 0, rows, low] = re[:, :mid]
                psi[k, 0, rows, high] = im[:, :mid]
                psi[k, 1, rows, low] = re[:, mid:]
                psi[k, 1, rows, high] = im[:, mid:]

    def right_backward(k):
        even = dot(psi[k, 0], table[LEFT[0]])
        odd = dot(psi[k, 1], table[LEFT[1]])
        for value, lanes in (((even + odd).astype(BF16), low), ((even - odd).astype(BF16), high)):
            for parity in range(2):
                rows = value[parity * mid : parity * mid + mid]
                half[k, parity, low, lanes] = rows[:, :mid]
                half[k, parity, high, lanes] = rows[:, mid:]

    def left_backward(k):
        for parity in range(2):
            field[k, parity] = dot(table[RIGHT[parity]], half[k, parity])

    def collect(k):
        for c in range(mid // CHUNK):
            even_re, odd_re = field[k, 0, span(c), :], field[k, 1, span(c), :]
            even_im, odd_im = field[k, 0, span(c, mid), :], field[k, 1, span(c, mid), :]
            for rows, re, im in (
                (span(c), even_re + odd_re, even_im + odd_im),
                (span(c, mid), even_re - odd_re, even_im - odd_im),
            ):
                p_re, p_im = probe[0, k, rows, :], probe[1, k, rows, :]
                add_re = p_re * re + p_im * im
                add_im = p_re * im - p_im * re
                if k == 0:
                    term[0, rows, :] = add_re
                    term[1, rows, :] = add_im
                else:
                    term[0, rows, :] += add_re
                    term[1, rows, :] += add_im
                o_re, o_im = obj[0, rows, :], obj[1, rows, :]
                keep[k, rows, :] += o_re * re + o_im * im
                send[k, rows, :] += o_re * im - o_im * re

    def turn_patch():
        for c in range(width // CHUNK):
            for lanes in (low, high):
                re, im = obj[0, span(c), lanes], obj[1, span(c), lanes]
                obj[0, span(c), lanes] = jnp.where(turn, re, -im)
                obj[1, span(c), lanes] = jnp.where(turn, im, re)

    def add_term():
        for c in range(width // CHUNK):
            target = pl.ds(row + c * CHUNK, CHUNK)
            for p in range(2):
                first = pltpu.roll(term[p, span(c), low], shift, 1)
                second = pltpu.roll(term[p, span(c), high], shift, 1)
                totals[p, block, target, :] += jnp.where(at_or_after, first, 0.0)
                totals[p, block + 1, target, :] += jnp.where(at_or_after, second, first)
                totals[p, block + 2, target, :] += jnp.where(at_or_after, 0.0, second)

    gather_patch()
    make_psi(0)
    make_psi(1)
    for k in range(modes):
        right_forward(k)
        if k + 2 < modes:
            make_psi(k + 2)
        if k == modes - 2:
            turn_patch()
        if k >= 1:
            left_forward(k - 1)
    left_forward(modes - 1)
    make_ratio()
    make_chi(0)
    make_chi(1)
    for k in range(modes):
        right_backward(k)
        if k + 2 < modes:
            make_chi(k + 2)
        if k >= 1:
            left_backward(k - 1)
        if k >= 2:
            collect(k - 2)
    left_backward(modes - 1)
    collect(modes - 2)
    collect(modes - 1)
    add_term()


class Moves:
    def __init__(self, sems):
        self.sems = sems
        self.started = []

    def begin(self, source, target):
        move = pltpu.make_async_copy(source, target, self.sems.at[len(self.started)])
        move.start()
        self.started.append(move)

    def wait(self):
        for move in self.started:
            move.wait()


def visit_all(later, offsets, counts, tile_rows, tile_cols, ext, pat, *rest):
    width = pat.shape[1]
    margin = width // 2
    base_row = lax.axis_index(ROW) * tile_rows - margin
    base_col = lax.axis_index(COL) * tile_cols - margin

    def visit(number, carry):
        row = offsets[0, number] - base_row
        col = offsets[1, number] - base_col
        beyond = jnp.logical_or(row < margin, row + width > margin + tile_rows)

        @pl.when(beyond if later else jnp.logical_not(beyond))
        def _():
            one_slot(number, row, col, ext, pat, *rest)

        return carry

    lax.fori_loop(0, counts[0, 0], visit, 0)


def first_kernel(
    offsets, counts, tile, inner, outer, pat, probe, table,
    ext, totals, keep, send, obj, term, psi, half, field, ratio, sems,
):
    rows, cols = tile.shape[1:]
    margin = inner.shape[2]
    last = cols // LANES + 1
    core = lax.axis_index(CORE)
    middle = pl.ds(margin, rows)
    moves = Moves(sems)
    for j in range(1, last):
        moves.begin(tile.at[:, :, pl.ds((j - 1) * LANES, LANES)], ext.at[:, j, middle, :])
    moves.begin(inner, ext.at[:, (1 - core) * last, middle, :])
    moves.begin(outer, ext.at[:, core * last, middle, :])
    totals[...] = jnp.zeros_like(totals)
    keep[...] = jnp.zeros_like(keep)
    send[...] = jnp.zeros_like(send)
    moves.wait()
    work = (obj, term, psi, half, field, ratio)
    visit_all(False, offsets, counts, rows, cols, ext, pat, probe, table, totals, keep, send, work)


def second_kernel(
    offsets, counts, above, below, corner_above, corner_below, ext_in, totals_in, keep_in,
    send_in, pat, probe, table,
    totals, keep, send, inner_ends, outer_ends,
    ext, obj, term, psi, half, field, ratio, sems,
):
    margin, cols = above.shape[1:]
    last = ext.shape[1] - 1
    rows = ext.shape[2] - 2 * margin
    core = lax.axis_index(CORE)
    inner_block, outer_block = (1 - core) * last, core * last
    top, middle, bottom = pl.ds(0, margin), pl.ds(margin, rows), pl.ds(margin + rows, margin)
    moves = Moves(sems)
    moves.begin(ext_in.at[:, :, middle, :], ext.at[:, :, middle, :])
    for j in range(1, last):
        lanes = pl.ds((j - 1) * LANES, LANES)
        moves.begin(above.at[:, :, lanes], ext.at[:, j, top, :])
        moves.begin(below.at[:, :, lanes], ext.at[:, j, bottom, :])
    for n, j in enumerate((inner_block, outer_block)):
        lanes = pl.ds(n * margin, margin)
        moves.begin(corner_above.at[:, :, lanes], ext.at[:, j, top, :])
        moves.begin(corner_below.at[:, :, lanes], ext.at[:, j, bottom, :])
    totals[...] = totals_in[...]
    keep[...] = keep_in[...]
    send[...] = send_in[...]
    moves.wait()
    work = (obj, term, psi, half, field, ratio)
    visit_all(True, offsets, counts, rows, cols, ext, pat, probe, table, totals, keep, send, work)
    moves = Moves(sems)
    for ends, j in ((outer_ends, outer_block), (inner_ends, inner_block)):
        moves.begin(totals.at[:, j, top, :], ends.at[:, pl.ds(0, margin), :])
        moves.begin(totals.at[:, j, bottom, :], ends.at[:, pl.ds(margin, margin), :])
    moves.wait()


def slot_scratch(modes, width):
    return [
        pltpu.VMEM((2, width, width), F32),
        pltpu.VMEM((2, width, width), F32),
        pltpu.VMEM((modes, 2, width, width), BF16),
        pltpu.VMEM((modes, 2, width, width), BF16),
        pltpu.VMEM((modes, 2, width, width), F32),
        pltpu.VMEM((2, width // 2, width), F32),
        pltpu.SemaphoreType.DMA((16,)),
    ]


def shapes(*dims):
    return [jax.ShapeDtypeStruct(shape, F32) for shape in dims]


def cost(slots, modes, width):
    return pl.CostEstimate(
        flops=slots * modes * width * width * width * 16,
        bytes_accessed=30 * MIB,
        transcendentals=slots * width * width,
    )


def first_slots(offsets, counts, tile, inner, outer, patterns, probe, table):
    modes, width = probe.shape[1:3]
    rows, cols = tile.shape[1:]
    grown = (2, cols // LANES + 2, rows + 2 * inner.shape[2], LANES)
    plane = (modes, width, width)
    return pl.pallas_call(
        first_kernel,
        out_shape=shapes(grown, grown, plane, plane),
        in_specs=[SMEM] * 2 + [FREE] * 3 + [VMEM] * 3,
        out_specs=[VMEM] * 4,
        scratch_shapes=slot_scratch(modes, width),
        compiler_params=pltpu.CompilerParams(vmem_limit_bytes=24 * MIB),
        cost_estimate=cost(4, modes, width),
        name="slots_first",
    )(offsets, counts, tile, inner, outer, patterns, probe, table)


def second_slots(offsets, counts, sides, ext, totals, keep, send, patterns, probe, table):
    modes, width = probe.shape[1:3]
    margin = sides[0].shape[1]
    ends = (2, 2 * margin, LANES)
    return pl.pallas_call(
        second_kernel,
        out_shape=shapes(totals.shape, keep.shape, send.shape, ends, ends),
        in_specs=[SMEM] * 2 + [FREE] * 5 + [VMEM] * 6,
        out_specs=[VMEM] * 3 + [FREE] * 2,
        scratch_shapes=[pltpu.VMEM(ext.shape, F32)] + slot_scratch(modes, width),
        input_output_aliases={7: 0, 8: 1, 9: 2},
        compiler_params=pltpu.CompilerParams(vmem_limit_bytes=24 * MIB),
        cost_estimate=cost(4, modes, width),
        name="slots_second",
    )(offsets, counts, *sides, ext, totals, keep, send, patterns, probe, table)


def prepare_kernel(patterns, probe, out, wide, moving):
    wide[...] = probe[...].astype(F32)
    slots, width = patterns.shape[:2]
    mid = width // 2
    source = lax.broadcasted_iota(jnp.int32, (width, width), 0)
    target = lax.broadcasted_iota(jnp.int32, (width, width), 1)
    wanted = jnp.where(target < mid, 2 * target, 2 * target - (width - 1))
    pick = (source == wanted).astype(BF16)

    def one(number, carry):
        value = patterns[number]
        total = None
        for _ in range(3):
            part = value.astype(BF16)
            value = value - part.astype(F32)
            moved = dot(part, pick)
            total = moved if total is None else total + moved
        for side in range(2):
            lanes = pl.ds(side * mid, mid)
            moving[side] = total[:, side * mid : side * mid + mid]
            for parity in range(2):
                out[number, pl.ds(parity * mid, mid), lanes] = moving[side, pl.ds(parity, mid, 2), :]
        return carry

    lax.fori_loop(0, slots, one, 0)


def prepare(patterns, probe):
    return pl.pallas_call(
        prepare_kernel,
        out_shape=shapes(patterns.shape, probe.shape),
        in_specs=[VMEM] * 2,
        out_specs=[VMEM] * 2,
        scratch_shapes=[pltpu.VMEM((2, patterns.shape[1], patterns.shape[2] // 2), F32)],
        compiler_params=pltpu.CompilerParams(vmem_limit_bytes=12 * MIB),
        cost_estimate=pl.CostEstimate(
            flops=patterns.size * 256 * 6, bytes_accessed=9 * MIB, transcendentals=0
        ),
        name="prepare",
    )(patterns, probe)


def cut_kernel(tile, top, bottom, inner, outer, sems):
    margin = top.shape[1]
    rows, cols = tile.shape[1:]
    core = lax.axis_index(CORE)

    def strip(start):
        return tile.at[:, :, pl.ds(pl.multiple_of(start, LANES), margin)]

    moves = Moves(sems)
    moves.begin(tile.at[:, pl.ds(rows - margin, margin), :], bottom)
    moves.begin(tile.at[:, pl.ds(0, margin), :], top)
    moves.begin(strip(core * (cols - margin)), outer)
    moves.begin(strip((1 - core) * (cols - margin)), inner)
    moves.wait()


def cut(tile, margin):
    rows, cols = tile.shape[1:]
    return pl.pallas_call(
        cut_kernel,
        out_shape=shapes((2, margin, cols), (2, margin, cols), (2, rows, margin), (2, rows, margin)),
        in_specs=[FREE],
        out_specs=[FREE] * 4,
        scratch_shapes=[pltpu.SemaphoreType.DMA((4,))],
        compiler_params=pltpu.CompilerParams(vmem_limit_bytes=MIB),
        cost_estimate=pl.CostEstimate(flops=0, bytes_accessed=4 * MIB, transcendentals=0),
        name="cut",
    )(tile)


def pair_kernel(keep, received, out, total, sems):
    sign = jnp.where(lax.axis_index(CORE) == 0, -1.0, 1.0).astype(F32)
    moves = Moves(sems)
    for k in range(keep.shape[0]):
        total[k] = keep[k] + received[k] * sign
        moves.begin(total.at[k], out.at[k])
    moves.wait()


def pair_sum(keep, received):
    return pl.pallas_call(
        pair_kernel,
        out_shape=jax.ShapeDtypeStruct(keep.shape, F32),
        in_specs=[VMEM] * 2,
        out_specs=FREE,
        scratch_shapes=[pltpu.VMEM(keep.shape, F32), pltpu.SemaphoreType.DMA((keep.shape[0],))],
        compiler_params=pltpu.CompilerParams(vmem_limit_bytes=8 * MIB),
        cost_estimate=pl.CostEstimate(flops=600_000, bytes_accessed=3 * MIB, transcendentals=0),
        name="pair_sum",
    )(keep, received)


def stash_kernel(totals, out, sems):
    moves = Moves(sems)
    for j in range(totals.shape[1]):
        moves.begin(totals.at[:, j], out.at[:, pl.ds(0, totals.shape[2]), pl.ds(j * LANES, LANES)])
    moves.wait()


def stash(totals):
    planes, blocks, rows, lanes = totals.shape
    return pl.pallas_call(
        stash_kernel,
        out_shape=jax.ShapeDtypeStruct((planes, SPARE * rows, blocks * lanes), F32),
        in_specs=[VMEM],
        out_specs=FREE,
        scratch_shapes=[pltpu.SemaphoreType.DMA((blocks,))],
        compiler_params=pltpu.CompilerParams(vmem_limit_bytes=6 * MIB),
        cost_estimate=pl.CostEstimate(flops=0, bytes_accessed=9 * MIB, transcendentals=0),
        name="stash",
    )(totals)


def add_sides(add, inner, outer, last):
    core = lax.axis_index(CORE)

    @pl.when(core == 0)
    def _():
        add(outer, 0)
        add(inner, last)

    @pl.when(core != 0)
    def _():
        add(inner, 0)
        add(outer, last)


def load(sources, targets, sems):
    moves = Moves(sems)
    for source, target in zip(sources, targets):
        moves.begin(source, target)
    moves.wait()


def turn_kernel(
    pieces_in, grown, inner_in, outer_in,
    copies_out, top_out, bottom_out, inner_out, outer_out,
    pieces, top, bottom, inner, outer, inner_side, outer_side, sems, out_sems,
):
    margin = top.shape[1]
    rows = inner_side.shape[1]
    cols = top.shape[2]
    core = lax.axis_index(CORE)
    center = pl.ds(LANES, cols)
    middle = pl.ds(margin, rows)

    def column(j):
        return pl.ds(pl.multiple_of(j * (cols + LANES), LANES), LANES)

    first = Moves(sems)
    first.begin(pieces_in, pieces)
    first.begin(inner_in, inner)
    first.begin(outer_in, outer)
    first.begin(grown.at[:, pl.ds(0, margin), center], top)
    first.begin(grown.at[:, pl.ds(margin + rows, margin), center], bottom)
    first.begin(grown.at[:, middle, column(1 - core)], inner_side)
    first.begin(grown.at[:, middle, column(core)], outer_side)
    first.wait()
    last = Moves(out_sems)
    last.begin(inner_side, inner_out)
    last.begin(outer_side, outer_out)

    def add(side, start):
        lanes = pl.ds(start, LANES)
        top[:, :, lanes] += side[:, :margin, :]
        bottom[:, :, lanes] += side[:, margin:, :]

    add_sides(add, inner, outer, cols - LANES)
    last.begin(top, top_out)
    last.begin(bottom, bottom_out)
    total = pieces[0]
    for n in range(1, pieces.shape[0]):
        total = total + pieces[n]
    for n in range(pieces.shape[0]):
        pieces[n] = total
    last.begin(pieces, copies_out)
    last.wait()


def turn(pieces, grown, inner, outer):
    margin = inner.shape[1] // 2
    rows, cols = grown.shape[1] // SPARE - 2 * margin, grown.shape[2] - 2 * LANES
    strip, side = (2, margin, cols), (2, rows, LANES)
    made = [pieces.shape, strip, strip, inner.shape, outer.shape, side, side]
    return pl.pallas_call(
        turn_kernel,
        out_shape=shapes(pieces.shape, strip, strip, side, side),
        in_specs=[FREE] * 4,
        out_specs=[FREE] * 5,
        scratch_shapes=[pltpu.VMEM(x, F32) for x in made]
        + [pltpu.SemaphoreType.DMA((7,)), pltpu.SemaphoreType.DMA((5,))],
        compiler_params=pltpu.CompilerParams(vmem_limit_bytes=8 * MIB),
        cost_estimate=pl.CostEstimate(flops=600_000, bytes_accessed=7 * MIB, transcendentals=0),
        name="turn",
    )(pieces, grown, inner, outer)


def finish_kernel(
    grown, inner_in, outer_in, above_in, below_in, out,
    center, inner, outer, above, below, sems,
):
    margin = above.shape[1]
    rows, cols = center.shape[1:]
    middle = grown.at[:, pl.ds(margin, rows), pl.ds(LANES, cols)]
    load(
        (middle, inner_in, outer_in, above_in, below_in),
        (center, inner, outer, above, below),
        sems,
    )
    moves = Moves(sems)
    for p in range(2):
        center[p, :margin, :] += above[p]
        center[p, rows - margin :, :] += below[p]

        def add(side, start):
            center[p, :, pl.ds(start, LANES)] += side[p]

        add_sides(add, inner, outer, cols - LANES)
        moves.begin(center.at[p], out.at[p])
    moves.wait()


def finish(grown, inner, outer, above, below):
    center = (2, inner.shape[1], above.shape[2])
    made = (center, inner.shape, outer.shape, above.shape, below.shape)
    return pl.pallas_call(
        finish_kernel,
        out_shape=jax.ShapeDtypeStruct(center, F32),
        in_specs=[FREE] * 5,
        out_specs=FREE,
        scratch_shapes=[pltpu.VMEM(x, F32) for x in made] + [pltpu.SemaphoreType.DMA((5,))],
        compiler_params=pltpu.CompilerParams(vmem_limit_bytes=8 * MIB),
        cost_estimate=pl.CostEstimate(flops=600_000, bytes_accessed=7 * MIB, transcendentals=0),
        name="finish",
    )(grown, inner, outer, above, below)


def join_kernel(own, other, out, sems):
    core = lax.axis_index(CORE)
    moves = Moves(sems)
    moves.begin(own, out.at[core])
    moves.begin(other, out.at[1 - core])
    moves.wait()


def join(own, other):
    return pl.pallas_call(
        join_kernel,
        out_shape=jax.ShapeDtypeStruct((2,) + own.shape, F32),
        in_specs=[FREE, FREE],
        out_specs=FREE,
        scratch_shapes=[pltpu.SemaphoreType.DMA((2,))],
        compiler_params=pltpu.CompilerParams(vmem_limit_bytes=MIB),
        cost_estimate=pl.CostEstimate(flops=0, bytes_accessed=4 * MIB, transcendentals=0),
        name="join",
    )(own, other)


def up(block, axes):
    count = lax.axis_size(axes)
    return lax.ppermute(block, axes, [(i, i + 1) for i in range(count - 1)])


def down(block, axes):
    count = lax.axis_size(axes)
    return lax.ppermute(block, axes, [(i + 1, i) for i in range(count - 1)])


def swap_inner(block, axes):
    count = lax.axis_size(axes)
    return lax.ppermute(block, axes, [(i, i ^ 1) for i in range(count)])


def swap_outer(block, axes):
    count = lax.axis_size(axes)
    pairs = [(i, i + 1) for i in range(1, count - 1, 2)]
    return lax.ppermute(block, axes, pairs + [(j, i) for i, j in pairs])


def exchange(counts, pieces):
    def send(given):
        return lax.all_to_all(given, CHIP, 0, 0, tiled=True)

    return lax.cond(counts[0, 0] > 0, send, jnp.zeros_like, pieces)


def on_device(object_field, probe, patterns, offsets, counts):
    rows = object_field.shape[1]
    width = patterns.shape[1]
    modes = probe.shape[1]
    margin = width // 2

    top, bottom, inner, outer = cut(object_field, margin)
    from_above = up(bottom, ROW)
    from_below = down(top, ROW)
    outer = swap_outer(outer, COL)
    inner = swap_inner(inner, COL)

    def corners(start):
        span = slice(start, start + margin)
        return jnp.concatenate([inner[:, span], outer[:, span]], axis=2)

    corner_above = up(corners(rows - margin), ROW)
    corner_below = down(corners(0), ROW)

    table = jnp.asarray(tables(width))
    measured, wide = prepare(patterns, probe)
    ext, totals, keep, send = first_slots(
        offsets, counts, object_field, inner, outer, measured, wide, table
    )
    sides = (from_above, from_below, corner_above, corner_below)
    totals, keep, send, inner_ends, outer_ends = second_slots(
        offsets, counts, sides, ext, totals, keep, send, measured, wide, table
    )

    received = swap_inner(send, COL)
    grown = stash(totals)
    received, grown = lax.optimization_barrier((received, grown))
    pair = pair_sum(keep, received)
    chips = lax.axis_size(CHIP)
    pieces = pair.reshape(chips, modes * width // chips, width)
    pieces = lax.all_to_all(pieces, CHIP, 0, 0, tiled=True)
    outer_ends = swap_outer(outer_ends, COL)
    inner_ends = swap_inner(inner_ends, COL)
    copies, top, bottom, inner, outer = turn(pieces, grown, inner_ends, outer_ends)
    from_above = up(bottom, ROW)
    from_below = down(top, ROW)
    outer = swap_outer(outer, COL)
    inner = swap_inner(inner, COL)
    gathered = exchange(counts, copies).reshape(modes, width, width)
    gathered, inner, outer, from_above, from_below = lax.optimization_barrier(
        (gathered, inner, outer, from_above, from_below)
    )
    other = swap_inner(gathered, COL)
    object_grad = finish(grown, inner, outer, from_above, from_below)
    return (object_grad, join(gathered, other))


def solution(mesh):
    rows, cols = mesh.devices.shape
    side = math.isqrt(rows)
    fine = Mesh(mesh.devices.reshape(side, side, cols // 2, 2), CHIP + (CORE,))
    in_specs = (P(None, ROW, COL), P(), P(ROW + COL, None, None), P(None, ROW + COL), P(ROW, COL))
    out_specs = (P(None, ROW, COL), P())
    return jax.shard_map(
        on_device, mesh=fine, in_specs=in_specs, out_specs=out_specs, check_vma=False
    )
```

```python
import math

import jax
import jax.numpy as jnp
import numpy as np
from jax import lax
from jax.experimental import pallas as pl
from jax.experimental.pallas import tpu as pltpu
from jax.sharding import Mesh, PartitionSpec as P

LANES = 128
CHUNK = 32
F32 = jnp.float32
BF16 = jnp.bfloat16
RIGHT = (0, 2)
LEFT = (1, 3)
MIB = 1024 * 1024
SPARE = 15
FREE = pl.BlockSpec(memory_space=pl.ANY)
VMEM = pl.BlockSpec(memory_space=pltpu.VMEM)
ROW, COL, CORE = ("x", "y"), ("z", "core"), "core"
CHIP = ("x", "y", "z")
SMEM = pl.BlockSpec(memory_space=pltpu.SMEM)


def tables(length):
    index = np.arange(length // 2)
    parts = []
    for parity in range(2):
        product = index[:, None] * (2 * index[None, :] + parity) % length
        angle = product * (2.0 * math.pi / length)
        factor = 1.0 / math.sqrt(length)
        re = (np.cos(angle) * factor).astype(BF16)
        im = (-np.sin(angle) * factor).astype(BF16)
        right = np.block([[re, im], [-im, re]])
        parts += [right, right.T]
    return np.stack(parts).astype(BF16)


def dot(a, b):
    return jnp.dot(a, b, preferred_element_type=F32)


def one_slot(number, row, col, ext, pat, probe, table, totals, keep, send, work):
    obj, psi, half, field = work
    width = pat.shape[1]
    modes = probe.shape[1]
    mid = width // 2
    blocks = ext.shape[1] - 2
    core = lax.axis_index(CORE)
    block = jnp.minimum(col // LANES, blocks - 1)
    rest = col - block * LANES
    back_shift = lax.rem(LANES - rest, LANES)
    shift = lax.rem(rest, LANES)
    lane = lax.broadcasted_iota(jnp.int32, (CHUNK, LANES), 1)
    from_first = lane < LANES - rest
    at_or_after = lane >= rest
    turn = (core + jnp.zeros((CHUNK, LANES), jnp.int32)) == 0
    low, high = pl.ds(0, mid), pl.ds(mid, mid)

    def span(c, base=0):
        return pl.ds(base + c * CHUNK, CHUNK)

    def gather_patch():
        for c in range(width // CHUNK):
            source = pl.ds(row + c * CHUNK, CHUNK)
            patch = []
            for p in range(2):
                parts = [
                    pltpu.roll(ext[p, block + j, source, :], back_shift, 1) for j in range(3)
                ]
                patch.append(
                    [
                        jnp.where(from_first, parts[0], parts[1]),
                        jnp.where(from_first, parts[1], parts[2]),
                    ]
                )
            for side, lanes in enumerate((low, high)):
                re, im = patch[0][side], patch[1][side]
                obj[0, span(c), lanes] = jnp.where(turn, re, -im)
                obj[1, span(c), lanes] = jnp.where(turn, im, re)
            for k in range(modes):
                waves = []
                for side, lanes in enumerate((low, high)):
                    o_re, o_im = patch[0][side], patch[1][side]
                    p_re, p_im = probe[0, k, span(c), lanes], probe[1, k, span(c), lanes]
                    waves.append((p_re * o_re - p_im * o_im, p_re * o_im + p_im * o_re))
                for part, lanes in enumerate((low, high)):
                    a, b = waves[0][part], waves[1][part]
                    psi[k, 0, span(c), lanes] = (a + b).astype(BF16)
                    psi[k, 1, span(c), lanes] = (a - b).astype(BF16)

    def right_forward_all():
        for parity, lanes in enumerate((low, high)):
            whole = dot(psi[:, parity].reshape(modes * width, width), table[RIGHT[parity]])
            for k in range(modes):
                right_forward(k, lanes, whole[k * width : (k + 1) * width])

    def right_forward(k, lanes, y):
        top, bottom = y[:mid], y[mid:]
        total, difference = (top + bottom).astype(BF16), (top - bottom).astype(BF16)
        half[k, 0, low, lanes] = total[:, :mid]
        half[k, 0, high, lanes] = total[:, mid:]
        half[k, 1, low, lanes] = difference[:, :mid]
        half[k, 1, high, lanes] = difference[:, mid:]

    def left_forward(k):
        for parity in range(2):
            field[k, parity] = dot(table[LEFT[parity]], half[k, parity])

    def make_all_chi():
        for parity in range(2):
            for c in range(mid // CHUNK):
                values = [
                    (field[k, parity, span(c), :], field[k, parity, span(c, mid), :])
                    for k in range(modes)
                ]
                total = None
                for re, im in values:
                    square = re * re + im * im
                    total = square if total is None else total + square
                measured = pat[number, span(c, parity * mid), :]
                scale = 1.0 - measured * lax.rsqrt(jnp.maximum(total, 1.0))
                rows = span(c, parity * mid)
                for k, (re, im) in enumerate(values):
                    re, im = (re * scale).astype(BF16), (im * scale).astype(BF16)
                    psi[k, 0, rows, low] = re[:, :mid]
                    psi[k, 0, rows, high] = im[:, :mid]
                    psi[k, 1, rows, low] = re[:, mid:]
                    psi[k, 1, rows, high] = im[:, mid:]

    def right_backward_all():
        evens = dot(psi[:, 0].reshape(modes * width, width), table[LEFT[0]])
        odds = dot(psi[:, 1].reshape(modes * width, width), table[LEFT[1]])
        for k in range(modes):
            right_backward(k, evens[k * width : (k + 1) * width], odds[k * width : (k + 1) * width])

    def right_backward(k, even, odd):
        for value, lanes in (((even + odd).astype(BF16), low), ((even - odd).astype(BF16), high)):
            for parity in range(2):
                rows = value[parity * mid : parity * mid + mid]
                half[k, parity, low, lanes] = rows[:, :mid]
                half[k, parity, high, lanes] = rows[:, mid:]

    def left_backward(k):
        for parity in range(2):
            field[k, parity] = dot(table[RIGHT[parity]], half[k, parity])

    def collect_all():
        for c in range(mid // CHUNK):
            for top in range(2):
                rows = span(c, top * mid)
                target = pl.ds(row + top * mid + c * CHUNK, CHUNK)
                o_re, o_im = obj[0, rows, :], obj[1, rows, :]
                sums = [None, None]
                for k in range(modes):
                    even_re, odd_re = field[k, 0, span(c), :], field[k, 1, span(c), :]
                    even_im, odd_im = field[k, 0, span(c, mid), :], field[k, 1, span(c, mid), :]
                    re = even_re - odd_re if top else even_re + odd_re
                    im = even_im - odd_im if top else even_im + odd_im
                    p_re, p_im = probe[0, k, rows, :], probe[1, k, rows, :]
                    adds = (p_re * re + p_im * im, p_re * im - p_im * re)
                    sums = [x if k == 0 else t + x for t, x in zip(sums, adds)]
                    keep[k, rows, :] += o_re * re + o_im * im
                    send[k, rows, :] += o_re * im - o_im * re
                for p in range(2):
                    first = pltpu.roll(sums[p][:, :LANES], shift, 1)
                    second = pltpu.roll(sums[p][:, LANES:], shift, 1)
                    totals[p, block, target, :] += jnp.where(at_or_after, first, 0.0)
                    totals[p, block + 1, target, :] += jnp.where(at_or_after, second, first)
                    totals[p, block + 2, target, :] += jnp.where(at_or_after, 0.0, second)

    gather_patch()
    right_forward_all()
    for k in range(modes):
        left_forward(k)
    make_all_chi()
    right_backward_all()
    for k in range(modes):
        left_backward(k)
    collect_all()


class Moves:
    def __init__(self, sems):
        self.sems = sems
        self.started = []

    def begin(self, source, target):
        move = pltpu.make_async_copy(source, target, self.sems.at[len(self.started)])
        move.start()
        self.started.append(move)

    def wait(self):
        for move in self.started:
            move.wait()


def visit_all(later, offsets, counts, tile_rows, tile_cols, ext, pat, *rest):
    width = pat.shape[1]
    margin = width // 2
    base_row = lax.axis_index(ROW) * tile_rows - margin
    base_col = lax.axis_index(COL) * tile_cols - margin

    def visit(number, carry):
        row = offsets[0, number] - base_row
        col = offsets[1, number] - base_col
        beyond = jnp.logical_or(row < margin, row + width > margin + tile_rows)

        @pl.when(beyond if later else jnp.logical_not(beyond))
        def _():
            one_slot(number, row, col, ext, pat, *rest)

        return carry

    lax.fori_loop(0, counts[0, 0], visit, 0)


def first_kernel(
    offsets, counts, tile, inner, outer, pat, probe, table,
    ext, totals, keep, send, obj, psi, half, field, sems,
):
    rows, cols = tile.shape[1:]
    margin = inner.shape[2]
    last = cols // LANES + 1
    core = lax.axis_index(CORE)
    middle = pl.ds(margin, rows)
    moves = Moves(sems)
    for j in range(1, last):
        moves.begin(tile.at[:, :, pl.ds((j - 1) * LANES, LANES)], ext.at[:, j, middle, :])
    moves.begin(inner, ext.at[:, (1 - core) * last, middle, :])
    moves.begin(outer, ext.at[:, core * last, middle, :])
    totals[...] = jnp.zeros_like(totals)
    keep[...] = jnp.zeros_like(keep)
    send[...] = jnp.zeros_like(send)
    moves.wait()
    work = (obj, psi, half, field)
    visit_all(False, offsets, counts, rows, cols, ext, pat, probe, table, totals, keep, send, work)


def second_kernel(
    offsets, counts, above, below, corner_above, corner_below, ext_in, totals_in, keep_in,
    send_in, pat, probe, table,
    totals, keep, send, inner_out, outer_out,
    ext, obj, psi, half, field, sems,
):
    margin, cols = above.shape[1:]
    last = ext.shape[1] - 1
    rows = ext.shape[2] - 2 * margin
    core = lax.axis_index(CORE)
    inner_block, outer_block = (1 - core) * last, core * last
    top, middle, bottom = pl.ds(0, margin), pl.ds(margin, rows), pl.ds(margin + rows, margin)
    moves = Moves(sems)
    moves.begin(ext_in.at[:, :, middle, :], ext.at[:, :, middle, :])
    for j in range(1, last):
        lanes = pl.ds((j - 1) * LANES, LANES)
        moves.begin(above.at[:, :, lanes], ext.at[:, j, top, :])
        moves.begin(below.at[:, :, lanes], ext.at[:, j, bottom, :])
    for n, j in enumerate((inner_block, outer_block)):
        lanes = pl.ds(n * margin, margin)
        moves.begin(corner_above.at[:, :, lanes], ext.at[:, j, top, :])
        moves.begin(corner_below.at[:, :, lanes], ext.at[:, j, bottom, :])
    totals[...] = totals_in[...]
    keep[...] = keep_in[...]
    send[...] = send_in[...]
    moves.wait()
    work = (obj, psi, half, field)
    visit_all(True, offsets, counts, rows, cols, ext, pat, probe, table, totals, keep, send, work)
    moves = Moves(sems)
    moves.begin(totals.at[:, outer_block], outer_out)
    moves.begin(totals.at[:, inner_block], inner_out)
    moves.wait()


def slot_scratch(modes, width):
    return [
        pltpu.VMEM((2, width, width), F32),
        pltpu.VMEM((modes, 2, width, width), BF16),
        pltpu.VMEM((modes, 2, width, width), BF16),
        pltpu.VMEM((modes, 2, width, width), F32),
        pltpu.SemaphoreType.DMA((16,)),
    ]


def shapes(*dims):
    return [jax.ShapeDtypeStruct(shape, F32) for shape in dims]


def cost(slots, modes, width):
    return pl.CostEstimate(
        flops=slots * modes * width * width * width * 16,
        bytes_accessed=30 * MIB,
        transcendentals=slots * width * width,
    )


def first_slots(offsets, counts, tile, inner, outer, patterns, probe, table):
    modes, width = probe.shape[1:3]
    rows, cols = tile.shape[1:]
    grown = (2, cols // LANES + 2, rows + 2 * inner.shape[2], LANES)
    plane = (modes, width, width)
    return pl.pallas_call(
        first_kernel,
        out_shape=shapes(grown, grown, plane, plane),
        in_specs=[SMEM] * 2 + [FREE] * 3 + [VMEM] * 3,
        out_specs=[VMEM] * 4,
        scratch_shapes=slot_scratch(modes, width),
        compiler_params=pltpu.CompilerParams(vmem_limit_bytes=24 * MIB),
        cost_estimate=cost(4, modes, width),
        name="slots_first",
    )(offsets, counts, tile, inner, outer, patterns, probe, table)


def second_slots(offsets, counts, sides, ext, totals, keep, send, patterns, probe, table):
    modes, width = probe.shape[1:3]
    margin = sides[0].shape[1]
    side = (2, ext.shape[2], LANES)
    return pl.pallas_call(
        second_kernel,
        out_shape=shapes(totals.shape, keep.shape, send.shape, side, side),
        in_specs=[SMEM] * 2 + [FREE] * 5 + [VMEM] * 6,
        out_specs=[VMEM] * 3 + [FREE] * 2,
        scratch_shapes=[pltpu.VMEM(ext.shape, F32)] + slot_scratch(modes, width),
        input_output_aliases={7: 0, 8: 1, 9: 2},
        compiler_params=pltpu.CompilerParams(vmem_limit_bytes=24 * MIB),
        cost_estimate=cost(4, modes, width),
        name="slots_second",
    )(offsets, counts, *sides, ext, totals, keep, send, patterns, probe, table)


def prepare_kernel(patterns, probe, out, wide, moving):
    wide[...] = probe[...].astype(F32)
    slots, width = patterns.shape[:2]
    mid = width // 2
    source = lax.broadcasted_iota(jnp.int32, (width, width), 0)
    target = lax.broadcasted_iota(jnp.int32, (width, width), 1)
    wanted = jnp.where(target < mid, 2 * target, 2 * target - (width - 1))
    pick = (source == wanted).astype(BF16)

    def one(number, carry):
        value = patterns[number]
        total = None
        for _ in range(2):
            part = value.astype(BF16)
            value = value - part.astype(F32)
            moved = dot(part, pick)
            total = moved if total is None else total + moved
        for side in range(2):
            lanes = pl.ds(side * mid, mid)
            moving[side] = total[:, side * mid : side * mid + mid]
            for parity in range(2):
                out[number, pl.ds(parity * mid, mid), lanes] = moving[side, pl.ds(parity, mid, 2), :]
        return carry

    lax.fori_loop(0, slots, one, 0)


def prepare(patterns, probe):
    return pl.pallas_call(
        prepare_kernel,
        out_shape=shapes(patterns.shape, probe.shape),
        in_specs=[VMEM] * 2,
        out_specs=[VMEM] * 2,
        scratch_shapes=[pltpu.VMEM((2, patterns.shape[1], patterns.shape[2] // 2), F32)],
        compiler_params=pltpu.CompilerParams(vmem_limit_bytes=12 * MIB),
        cost_estimate=pl.CostEstimate(
            flops=patterns.size * 256 * 6, bytes_accessed=9 * MIB, transcendentals=0
        ),
        name="prepare",
    )(patterns, probe)


def cut_kernel(tile, top, bottom, inner, outer, sems):
    margin = top.shape[1]
    rows, cols = tile.shape[1:]
    core = lax.axis_index(CORE)

    def strip(start):
        return tile.at[:, :, pl.ds(pl.multiple_of(start, LANES), margin)]

    moves = Moves(sems)
    moves.begin(tile.at[:, pl.ds(rows - margin, margin), :], bottom)
    moves.begin(tile.at[:, pl.ds(0, margin), :], top)
    moves.begin(strip(core * (cols - margin)), outer)
    moves.begin(strip((1 - core) * (cols - margin)), inner)
    moves.wait()


def cut(tile, margin):
    rows, cols = tile.shape[1:]
    return pl.pallas_call(
        cut_kernel,
        out_shape=shapes((2, margin, cols), (2, margin, cols), (2, rows, margin), (2, rows, margin)),
        in_specs=[FREE],
        out_specs=[FREE] * 4,
        scratch_shapes=[pltpu.SemaphoreType.DMA((4,))],
        compiler_params=pltpu.CompilerParams(vmem_limit_bytes=MIB),
        cost_estimate=pl.CostEstimate(flops=0, bytes_accessed=4 * MIB, transcendentals=0),
        name="cut",
    )(tile)


def pair_kernel(keep, received, out, total, sems):
    sign = jnp.where(lax.axis_index(CORE) == 0, -1.0, 1.0).astype(F32)
    moves = Moves(sems)
    for k in range(keep.shape[0]):
        total[k] = keep[k] + received[k] * sign
        moves.begin(total.at[k], out.at[k])
    moves.wait()


def pair_sum(keep, received):
    return pl.pallas_call(
        pair_kernel,
        out_shape=jax.ShapeDtypeStruct(keep.shape, F32),
        in_specs=[VMEM] * 2,
        out_specs=FREE,
        scratch_shapes=[pltpu.VMEM(keep.shape, F32), pltpu.SemaphoreType.DMA((keep.shape[0],))],
        compiler_params=pltpu.CompilerParams(vmem_limit_bytes=8 * MIB),
        cost_estimate=pl.CostEstimate(flops=600_000, bytes_accessed=3 * MIB, transcendentals=0),
        name="pair_sum",
    )(keep, received)


def stash_kernel(totals, out, sems):
    moves = Moves(sems)
    for j in range(totals.shape[1]):
        moves.begin(totals.at[:, j], out.at[:, pl.ds(0, totals.shape[2]), pl.ds(j * LANES, LANES)])
    moves.wait()


def stash(totals):
    planes, blocks, rows, lanes = totals.shape
    return pl.pallas_call(
        stash_kernel,
        out_shape=jax.ShapeDtypeStruct((planes, SPARE * rows, blocks * lanes), F32),
        in_specs=[VMEM],
        out_specs=FREE,
        scratch_shapes=[pltpu.SemaphoreType.DMA((blocks,))],
        compiler_params=pltpu.CompilerParams(vmem_limit_bytes=6 * MIB),
        cost_estimate=pl.CostEstimate(flops=0, bytes_accessed=9 * MIB, transcendentals=0),
        name="stash",
    )(totals)


def add_sides(add, inner, outer, last):
    core = lax.axis_index(CORE)

    @pl.when(core == 0)
    def _():
        add(outer, 0)
        add(inner, last)

    @pl.when(core != 0)
    def _():
        add(inner, 0)
        add(outer, last)


def load(sources, targets, sems):
    moves = Moves(sems)
    for source, target in zip(sources, targets):
        moves.begin(source, target)
    moves.wait()


def turn_kernel(
    pieces_in, grown, inner_in, outer_in, copies_out, top_out, bottom_out,
    pieces, top, bottom, inner, outer, sems, out_sems,
):
    margin, cols = top.shape[1:]
    rows = inner_in.shape[1] - 2 * margin
    low, high = pl.ds(0, margin), pl.ds(margin + rows, margin)
    center = pl.ds(LANES, cols)
    first = Moves(sems)
    first.begin(pieces_in, pieces)
    for side_in, side in ((inner_in, inner), (outer_in, outer)):
        first.begin(side_in.at[:, low, :], side.at[:, low, :])
        first.begin(side_in.at[:, high, :], side.at[:, pl.ds(margin, margin), :])
    first.begin(grown.at[:, low, center], top)
    first.begin(grown.at[:, high, center], bottom)
    first.wait()
    last = Moves(out_sems)

    def add(side, start):
        lanes = pl.ds(start, LANES)
        top[:, :, lanes] += side[:, :margin, :]
        bottom[:, :, lanes] += side[:, margin:, :]

    add_sides(add, inner, outer, cols - LANES)
    last.begin(top, top_out)
    last.begin(bottom, bottom_out)
    total = pieces[0]
    for n in range(1, pieces.shape[0]):
        total = total + pieces[n]
    for n in range(pieces.shape[0]):
        pieces[n] = total
    last.begin(pieces, copies_out)
    last.wait()


def turn(pieces, grown, inner, outer):
    margin = inner.shape[2]
    strip, ends = (2, margin, grown.shape[2] - 2 * LANES), (2, 2 * margin, margin)
    return pl.pallas_call(
        turn_kernel,
        out_shape=shapes(pieces.shape, strip, strip),
        in_specs=[FREE] * 4,
        out_specs=[FREE] * 3,
        scratch_shapes=[pltpu.VMEM(x, F32) for x in (pieces.shape, strip, strip, ends, ends)]
        + [pltpu.SemaphoreType.DMA((7,)), pltpu.SemaphoreType.DMA((3,))],
        compiler_params=pltpu.CompilerParams(vmem_limit_bytes=8 * MIB),
        cost_estimate=pl.CostEstimate(flops=600_000, bytes_accessed=7 * MIB, transcendentals=0),
        name="turn",
    )(pieces, grown, inner, outer)


def finish_kernel(
    grown, inner_in, outer_in, above_in, below_in, out,
    center, inner, outer, above, below, sems,
):
    margin = above.shape[1]
    rows, cols = center.shape[1:]
    middle = pl.ds(margin, rows)
    core_part = grown.at[:, middle, pl.ds(LANES, cols)]
    load(
        (core_part, inner_in.at[:, middle], outer_in.at[:, middle], above_in, below_in),
        (center, inner, outer, above, below),
        sems,
    )
    moves = Moves(sems)
    for p in range(2):
        center[p, :margin, :] += above[p]
        center[p, rows - margin :, :] += below[p]

        def add(side, start):
            center[p, :, pl.ds(start, LANES)] += side[p]

        add_sides(add, inner, outer, cols - LANES)
        moves.begin(center.at[p], out.at[p])
    moves.wait()


def finish(grown, inner, outer, above, below):
    center = (2, inner.shape[1] - 2 * above.shape[1], above.shape[2])
    side = (2, center[1], LANES)
    made = (center, side, side, above.shape, below.shape)
    return pl.pallas_call(
        finish_kernel,
        out_shape=jax.ShapeDtypeStruct(center, F32),
        in_specs=[FREE] * 5,
        out_specs=FREE,
        scratch_shapes=[pltpu.VMEM(x, F32) for x in made] + [pltpu.SemaphoreType.DMA((5,))],
        compiler_params=pltpu.CompilerParams(vmem_limit_bytes=8 * MIB),
        cost_estimate=pl.CostEstimate(flops=600_000, bytes_accessed=7 * MIB, transcendentals=0),
        name="finish",
    )(grown, inner, outer, above, below)


def join_kernel(own, other, out, sems):
    core = lax.axis_index(CORE)
    moves = Moves(sems)
    moves.begin(own, out.at[core])
    moves.begin(other, out.at[1 - core])
    moves.wait()


def join(own, other):
    return pl.pallas_call(
        join_kernel,
        out_shape=jax.ShapeDtypeStruct((2,) + own.shape, F32),
        in_specs=[FREE, FREE],
        out_specs=FREE,
        scratch_shapes=[pltpu.SemaphoreType.DMA((2,))],
        compiler_params=pltpu.CompilerParams(vmem_limit_bytes=MIB),
        cost_estimate=pl.CostEstimate(flops=0, bytes_accessed=4 * MIB, transcendentals=0),
        name="join",
    )(own, other)


def up(block, axes):
    count = lax.axis_size(axes)
    return lax.ppermute(block, axes, [(i, i + 1) for i in range(count - 1)])


def down(block, axes):
    count = lax.axis_size(axes)
    return lax.ppermute(block, axes, [(i + 1, i) for i in range(count - 1)])


def swap_inner(block, axes):
    count = lax.axis_size(axes)
    return lax.ppermute(block, axes, [(i, i ^ 1) for i in range(count)])


def swap_outer(block, axes):
    count = lax.axis_size(axes)
    pairs = [(i, i + 1) for i in range(1, count - 1, 2)]
    return lax.ppermute(block, axes, pairs + [(j, i) for i, j in pairs])


def exchange(counts, pieces):
    def send(given):
        return lax.all_to_all(given, CHIP, 0, 0, tiled=True)

    return lax.cond(counts[0, 0] > 0, send, jnp.zeros_like, pieces)


def on_device(object_field, probe, patterns, offsets, counts):
    rows = object_field.shape[1]
    width = patterns.shape[1]
    modes = probe.shape[1]
    margin = width // 2

    top, bottom, inner, outer = cut(object_field, margin)
    from_above = up(bottom, ROW)
    from_below = down(top, ROW)
    outer = swap_outer(outer, COL)
    inner = swap_inner(inner, COL)

    def corners(start):
        span = slice(start, start + margin)
        return jnp.concatenate([inner[:, span], outer[:, span]], axis=2)

    corner_above = up(corners(rows - margin), ROW)
    corner_below = down(corners(0), ROW)

    table = jnp.asarray(tables(width))
    measured, wide = prepare(patterns, probe)
    ext, totals, keep, send = first_slots(
        offsets, counts, object_field, inner, outer, measured, wide, table
    )
    sides = (from_above, from_below, corner_above, corner_below)
    totals, keep, send, inner, outer = second_slots(
        offsets, counts, sides, ext, totals, keep, send, measured, wide, table
    )

    received = swap_inner(send, COL)
    outer = swap_outer(outer, COL)
    inner = swap_inner(inner, COL)
    grown = stash(totals)
    received, grown = lax.optimization_barrier((received, grown))
    pair = pair_sum(keep, received)
    chips = lax.axis_size(CHIP)
    pieces = exchange(counts, pair.reshape(chips, modes * width // chips, width))
    pieces, inner, outer = lax.optimization_barrier((pieces, inner, outer))
    copies, top, bottom = turn(pieces, grown, inner, outer)
    from_above = up(bottom, ROW)
    from_below = down(top, ROW)
    gathered = exchange(counts, copies).reshape(modes, width, width)
    gathered, from_above, from_below = lax.optimization_barrier((gathered, from_above, from_below))
    other = swap_inner(gathered, COL)
    object_grad = finish(grown, inner, outer, from_above, from_below)
    return (object_grad, join(gathered, other))


def solution(mesh):
    rows, cols = mesh.devices.shape
    side = math.isqrt(rows)
    fine = Mesh(mesh.devices.reshape(side, side, cols // 2, 2), CHIP + (CORE,))
    in_specs = (P(None, ROW, COL), P(), P(ROW + COL, None, None), P(None, ROW + COL), P(ROW, COL))
    out_specs = (P(None, ROW, COL), P())
    return jax.shard_map(
        on_device, mesh=fine, in_specs=in_specs, out_specs=out_specs, check_vma=False
    )
```

```python
import math

import jax
import jax.numpy as jnp
import numpy as np
from jax import lax
from jax.experimental import pallas as pl
from jax.experimental.pallas import tpu as pltpu
from jax.sharding import Mesh, PartitionSpec as P

LANES = 128
CHUNK = 32
F32 = jnp.float32
BF16 = jnp.bfloat16
RIGHT = (0, 2)
LEFT = (1, 3)
MIB = 1024 * 1024
SPARE = 15
FREE = pl.BlockSpec(memory_space=pl.ANY)
VMEM = pl.BlockSpec(memory_space=pltpu.VMEM)
ROW, COL, CORE = ("x", "y"), ("z", "core"), "core"
CHIP = ("x", "y", "z")
SMEM = pl.BlockSpec(memory_space=pltpu.SMEM)


def tables(length):
    index = np.arange(length // 2)
    parts = []
    for parity in range(2):
        product = index[:, None] * (2 * index[None, :] + parity) % length
        angle = product * (2.0 * math.pi / length)
        factor = 1.0 / math.sqrt(length)
        re = (np.cos(angle) * factor).astype(BF16)
        im = (-np.sin(angle) * factor).astype(BF16)
        right = np.block([[re, im], [-im, re]])
        parts += [right, right.T]
    return np.stack(parts).astype(BF16)


def dot(a, b):
    return jnp.dot(a, b, preferred_element_type=F32)


def one_slot(number, row, col, ext, pat, probe, table, totals, keep, send, work):
    obj, psi, half, field = work
    width = pat.shape[1]
    modes = probe.shape[1]
    mid = width // 2
    blocks = ext.shape[1] - 2
    core = lax.axis_index(CORE)
    block = jnp.minimum(col // LANES, blocks - 1)
    rest = col - block * LANES
    back_shift = lax.rem(LANES - rest, LANES)
    shift = lax.rem(rest, LANES)
    lane = lax.broadcasted_iota(jnp.int32, (CHUNK, LANES), 1)
    from_first = lane < LANES - rest
    at_or_after = lane >= rest
    turn = (core + jnp.zeros((CHUNK, LANES), jnp.int32)) == 0
    low, high = pl.ds(0, mid), pl.ds(mid, mid)

    def span(c, base=0):
        return pl.ds(base + c * CHUNK, CHUNK)

    def gather_patch():
        for c in range(width // CHUNK):
            source = pl.ds(row + c * CHUNK, CHUNK)
            patch = []
            for p in range(2):
                parts = [
                    pltpu.roll(ext[p, block + j, source, :], back_shift, 1) for j in range(3)
                ]
                patch.append(
                    [
                        jnp.where(from_first, parts[0], parts[1]),
                        jnp.where(from_first, parts[1], parts[2]),
                    ]
                )
            for side, lanes in enumerate((low, high)):
                re, im = patch[0][side], patch[1][side]
                obj[0, span(c), lanes] = jnp.where(turn, re, -im)
                obj[1, span(c), lanes] = jnp.where(turn, im, re)
            for k in range(modes):
                waves = []
                for side, lanes in enumerate((low, high)):
                    o_re, o_im = patch[0][side], patch[1][side]
                    p_re, p_im = probe[0, k, span(c), lanes], probe[1, k, span(c), lanes]
                    waves.append((p_re * o_re - p_im * o_im, p_re * o_im + p_im * o_re))
                for part, lanes in enumerate((low, high)):
                    a, b = waves[0][part], waves[1][part]
                    psi[k, 0, span(c), lanes] = (a + b).astype(BF16)
                    psi[k, 1, span(c), lanes] = (a - b).astype(BF16)

    def right_forward_all():
        for parity, lanes in enumerate((low, high)):
            whole = dot(psi[:, parity].reshape(modes * width, width), table[RIGHT[parity]])
            for k in range(modes):
                right_forward(k, lanes, whole[k * width : (k + 1) * width])

    def right_forward(k, lanes, y):
        top, bottom = y[:mid], y[mid:]
        total, difference = (top + bottom).astype(BF16), (top - bottom).astype(BF16)
        half[k, 0, low, lanes] = total[:, :mid]
        half[k, 0, high, lanes] = total[:, mid:]
        half[k, 1, low, lanes] = difference[:, :mid]
        half[k, 1, high, lanes] = difference[:, mid:]

    def left_forward(k):
        for parity in range(2):
            field[k, parity] = dot(table[LEFT[parity]], half[k, parity])

    def make_all_chi():
        for parity in range(2):
            for c in range(mid // CHUNK):
                values = [
                    (field[k, parity, span(c), :], field[k, parity, span(c, mid), :])
                    for k in range(modes)
                ]
                total = None
                for re, im in values:
                    square = re * re + im * im
                    total = square if total is None else total + square
                measured = pat[number, span(c, parity * mid), :]
                scale = 1.0 - measured * lax.rsqrt(jnp.maximum(total, 1.0))
                rows = span(c, parity * mid)
                for k, (re, im) in enumerate(values):
                    re, im = (re * scale).astype(BF16), (im * scale).astype(BF16)
                    psi[k, 0, rows, low] = re[:, :mid]
                    psi[k, 0, rows, high] = im[:, :mid]
                    psi[k, 1, rows, low] = re[:, mid:]
                    psi[k, 1, rows, high] = im[:, mid:]

    def right_backward_all():
        evens = dot(psi[:, 0].reshape(modes * width, width), table[LEFT[0]])
        odds = dot(psi[:, 1].reshape(modes * width, width), table[LEFT[1]])
        for k in range(modes):
            right_backward(k, evens[k * width : (k + 1) * width], odds[k * width : (k + 1) * width])

    def right_backward(k, even, odd):
        for value, lanes in (((even + odd).astype(BF16), low), ((even - odd).astype(BF16), high)):
            for parity in range(2):
                rows = value[parity * mid : parity * mid + mid]
                half[k, parity, low, lanes] = rows[:, :mid]
                half[k, parity, high, lanes] = rows[:, mid:]

    def left_backward(k):
        for parity in range(2):
            field[k, parity] = dot(table[RIGHT[parity]], half[k, parity])

    def collect_all():
        for c in range(mid // CHUNK):
            for top in range(2):
                rows = span(c, top * mid)
                target = pl.ds(row + top * mid + c * CHUNK, CHUNK)
                o_re, o_im = obj[0, rows, :], obj[1, rows, :]
                sums = [None, None]
                for k in range(modes):
                    even_re, odd_re = field[k, 0, span(c), :], field[k, 1, span(c), :]
                    even_im, odd_im = field[k, 0, span(c, mid), :], field[k, 1, span(c, mid), :]
                    re = even_re - odd_re if top else even_re + odd_re
                    im = even_im - odd_im if top else even_im + odd_im
                    p_re, p_im = probe[0, k, rows, :], probe[1, k, rows, :]
                    adds = (p_re * re + p_im * im, p_re * im - p_im * re)
                    sums = [x if k == 0 else t + x for t, x in zip(sums, adds)]
                    keep[k, rows, :] += o_re * re + o_im * im
                    send[k, rows, :] += o_re * im - o_im * re
                for p in range(2):
                    first = pltpu.roll(sums[p][:, :LANES], shift, 1)
                    second = pltpu.roll(sums[p][:, LANES:], shift, 1)
                    totals[p, block, target, :] += jnp.where(at_or_after, first, 0.0)
                    totals[p, block + 1, target, :] += jnp.where(at_or_after, second, first)
                    totals[p, block + 2, target, :] += jnp.where(at_or_after, 0.0, second)

    gather_patch()
    right_forward_all()
    for k in range(modes):
        left_forward(k)
    make_all_chi()
    right_backward_all()
    for k in range(modes):
        left_backward(k)
    collect_all()


class Moves:
    def __init__(self, sems):
        self.sems = sems
        self.started = []

    def begin(self, source, target):
        move = pltpu.make_async_copy(source, target, self.sems.at[len(self.started)])
        move.start()
        self.started.append(move)

    def wait(self):
        for move in self.started:
            move.wait()


def visit_all(later, offsets, counts, tile_rows, tile_cols, ext, pat, *rest):
    width = pat.shape[1]
    margin = width // 2
    base_row = lax.axis_index(ROW) * tile_rows - margin
    base_col = lax.axis_index(COL) * tile_cols - margin

    def visit(number, carry):
        row = offsets[0, number] - base_row
        col = offsets[1, number] - base_col
        beyond = jnp.logical_or(row < margin, row + width > margin + tile_rows)

        @pl.when(beyond if later else jnp.logical_not(beyond))
        def _():
            one_slot(number, row, col, ext, pat, *rest)

        return carry

    lax.fori_loop(0, counts[0, 0], visit, 0)


def first_kernel(
    offsets, counts, tile, inner, outer, pat, probe, table,
    ext, totals, keep, send, obj, psi, half, field, sems,
):
    rows, cols = tile.shape[1:]
    margin = inner.shape[2]
    last = cols // LANES + 1
    core = lax.axis_index(CORE)
    middle = pl.ds(margin, rows)
    moves = Moves(sems)
    for j in range(1, last):
        moves.begin(tile.at[:, :, pl.ds((j - 1) * LANES, LANES)], ext.at[:, j, middle, :])
    moves.begin(inner, ext.at[:, (1 - core) * last, middle, :])
    moves.begin(outer, ext.at[:, core * last, middle, :])
    totals[...] = jnp.zeros_like(totals)
    keep[...] = jnp.zeros_like(keep)
    send[...] = jnp.zeros_like(send)
    moves.wait()
    work = (obj, psi, half, field)
    visit_all(False, offsets, counts, rows, cols, ext, pat, probe, table, totals, keep, send, work)


def second_kernel(
    offsets, counts, near, far, corner_near, corner_far, ext_in, totals_in, keep_in,
    send_in, pat, probe, table,
    totals, keep, send, inner_out, outer_out,
    ext, obj, psi, half, field, sems,
):
    margin, cols = near.shape[1:]
    last = ext.shape[1] - 1
    rows = ext.shape[2] - 2 * margin
    core = lax.axis_index(CORE)
    inner_block, outer_block = (1 - core) * last, core * last
    middle = pl.ds(margin, rows)
    moves = Moves(sems)
    moves.begin(ext_in.at[:, :, middle, :], ext.at[:, :, middle, :])
    odd = odd_row()
    near_rows, far_rows = (
        pl.ds(pl.multiple_of(start, LANES), margin)
        for start in ((1 - odd) * (margin + rows), odd * (margin + rows))
    )
    for j in range(1, last):
        lanes = pl.ds((j - 1) * LANES, LANES)
        moves.begin(near.at[:, :, lanes], ext.at[:, j, near_rows, :])
        moves.begin(far.at[:, :, lanes], ext.at[:, j, far_rows, :])
    for n, j in enumerate((inner_block, outer_block)):
        lanes = pl.ds(n * margin, margin)
        moves.begin(corner_near.at[:, :, lanes], ext.at[:, j, near_rows, :])
        moves.begin(corner_far.at[:, :, lanes], ext.at[:, j, far_rows, :])
    totals[...] = totals_in[...]
    keep[...] = keep_in[...]
    send[...] = send_in[...]
    moves.wait()
    work = (obj, psi, half, field)
    visit_all(True, offsets, counts, rows, cols, ext, pat, probe, table, totals, keep, send, work)
    moves = Moves(sems)
    moves.begin(totals.at[:, outer_block], outer_out)
    moves.begin(totals.at[:, inner_block], inner_out)
    moves.wait()


def slot_scratch(modes, width):
    return [
        pltpu.VMEM((2, width, width), F32),
        pltpu.VMEM((modes, 2, width, width), BF16),
        pltpu.VMEM((modes, 2, width, width), BF16),
        pltpu.VMEM((modes, 2, width, width), F32),
        pltpu.SemaphoreType.DMA((16,)),
    ]


def shapes(*dims):
    return [jax.ShapeDtypeStruct(shape, F32) for shape in dims]


def cost(slots, modes, width):
    return pl.CostEstimate(
        flops=slots * modes * width * width * width * 16,
        bytes_accessed=30 * MIB,
        transcendentals=slots * width * width,
    )


def first_slots(offsets, counts, tile, inner, outer, patterns, probe, table):
    modes, width = probe.shape[1:3]
    rows, cols = tile.shape[1:]
    grown = (2, cols // LANES + 2, rows + 2 * inner.shape[2], LANES)
    plane = (modes, width, width)
    return pl.pallas_call(
        first_kernel,
        out_shape=shapes(grown, grown, plane, plane),
        in_specs=[SMEM] * 2 + [FREE] * 3 + [VMEM] * 3,
        out_specs=[VMEM] * 4,
        scratch_shapes=slot_scratch(modes, width),
        compiler_params=pltpu.CompilerParams(vmem_limit_bytes=24 * MIB),
        cost_estimate=cost(4, modes, width),
        name="slots_first",
    )(offsets, counts, tile, inner, outer, patterns, probe, table)


def second_slots(offsets, counts, sides, ext, totals, keep, send, patterns, probe, table):
    modes, width = probe.shape[1:3]
    margin = sides[0].shape[1]
    side = (2, ext.shape[2], LANES)
    return pl.pallas_call(
        second_kernel,
        out_shape=shapes(totals.shape, keep.shape, send.shape, side, side),
        in_specs=[SMEM] * 2 + [FREE] * 5 + [VMEM] * 6,
        out_specs=[VMEM] * 3 + [FREE] * 2,
        scratch_shapes=[pltpu.VMEM(ext.shape, F32)] + slot_scratch(modes, width),
        input_output_aliases={7: 0, 8: 1, 9: 2},
        compiler_params=pltpu.CompilerParams(vmem_limit_bytes=24 * MIB),
        cost_estimate=cost(4, modes, width),
        name="slots_second",
    )(offsets, counts, *sides, ext, totals, keep, send, patterns, probe, table)


def prepare_kernel(patterns, probe, out, wide, moving):
    wide[...] = probe[...].astype(F32)
    slots, width = patterns.shape[:2]
    mid = width // 2
    source = lax.broadcasted_iota(jnp.int32, (width, width), 0)
    target = lax.broadcasted_iota(jnp.int32, (width, width), 1)
    wanted = jnp.where(target < mid, 2 * target, 2 * target - (width - 1))
    pick = (source == wanted).astype(BF16)

    def one(number, carry):
        value = patterns[number]
        total = None
        for _ in range(2):
            part = value.astype(BF16)
            value = value - part.astype(F32)
            moved = dot(part, pick)
            total = moved if total is None else total + moved
        for side in range(2):
            lanes = pl.ds(side * mid, mid)
            moving[side] = total[:, side * mid : side * mid + mid]
            for parity in range(2):
                out[number, pl.ds(parity * mid, mid), lanes] = moving[side, pl.ds(parity, mid, 2), :]
        return carry

    lax.fori_loop(0, slots, one, 0)


def prepare(patterns, probe):
    return pl.pallas_call(
        prepare_kernel,
        out_shape=shapes(patterns.shape, probe.shape),
        in_specs=[VMEM] * 2,
        out_specs=[VMEM] * 2,
        scratch_shapes=[pltpu.VMEM((2, patterns.shape[1], patterns.shape[2] // 2), F32)],
        compiler_params=pltpu.CompilerParams(vmem_limit_bytes=12 * MIB),
        cost_estimate=pl.CostEstimate(
            flops=patterns.size * 256 * 6, bytes_accessed=9 * MIB, transcendentals=0
        ),
        name="prepare",
    )(patterns, probe)


def odd_row():
    return lax.rem(lax.axis_index(ROW), 2)


def cut_kernel(tile, near, far, inner, outer, sems):
    margin = near.shape[1]
    rows, cols = tile.shape[1:]
    core = lax.axis_index(CORE)
    odd = odd_row()

    def band(start):
        return tile.at[:, pl.ds(pl.multiple_of(start, LANES), margin), :]

    def strip(start):
        return tile.at[:, :, pl.ds(pl.multiple_of(start, LANES), margin)]

    moves = Moves(sems)
    moves.begin(band((1 - odd) * (rows - margin)), near)
    moves.begin(band(odd * (rows - margin)), far)
    moves.begin(strip(core * (cols - margin)), outer)
    moves.begin(strip((1 - core) * (cols - margin)), inner)
    moves.wait()


def cut(tile, margin):
    rows, cols = tile.shape[1:]
    return pl.pallas_call(
        cut_kernel,
        out_shape=shapes((2, margin, cols), (2, margin, cols), (2, rows, margin), (2, rows, margin)),
        in_specs=[FREE],
        out_specs=[FREE] * 4,
        scratch_shapes=[pltpu.SemaphoreType.DMA((4,))],
        compiler_params=pltpu.CompilerParams(vmem_limit_bytes=MIB),
        cost_estimate=pl.CostEstimate(flops=0, bytes_accessed=4 * MIB, transcendentals=0),
        name="cut",
    )(tile)


def pair_kernel(keep, received, out, total, sems):
    sign = jnp.where(lax.axis_index(CORE) == 0, -1.0, 1.0).astype(F32)
    moves = Moves(sems)
    for k in range(keep.shape[0]):
        total[k] = keep[k] + received[k] * sign
        moves.begin(total.at[k], out.at[k])
    moves.wait()


def pair_sum(keep, received):
    return pl.pallas_call(
        pair_kernel,
        out_shape=jax.ShapeDtypeStruct(keep.shape, F32),
        in_specs=[VMEM] * 2,
        out_specs=FREE,
        scratch_shapes=[pltpu.VMEM(keep.shape, F32), pltpu.SemaphoreType.DMA((keep.shape[0],))],
        compiler_params=pltpu.CompilerParams(vmem_limit_bytes=8 * MIB),
        cost_estimate=pl.CostEstimate(flops=600_000, bytes_accessed=3 * MIB, transcendentals=0),
        name="pair_sum",
    )(keep, received)


def stash_kernel(totals, out, sems):
    moves = Moves(sems)
    for j in range(totals.shape[1]):
        moves.begin(totals.at[:, j], out.at[:, pl.ds(0, totals.shape[2]), pl.ds(j * LANES, LANES)])
    moves.wait()


def stash(totals):
    planes, blocks, rows, lanes = totals.shape
    return pl.pallas_call(
        stash_kernel,
        out_shape=jax.ShapeDtypeStruct((planes, SPARE * rows, blocks * lanes), F32),
        in_specs=[VMEM],
        out_specs=FREE,
        scratch_shapes=[pltpu.SemaphoreType.DMA((blocks,))],
        compiler_params=pltpu.CompilerParams(vmem_limit_bytes=6 * MIB),
        cost_estimate=pl.CostEstimate(flops=0, bytes_accessed=9 * MIB, transcendentals=0),
        name="stash",
    )(totals)


def corners_kernel(inner, outer, near, far, sems):
    margin = near.shape[1]
    start = inner.shape[1] - margin
    odd = odd_row()
    moves = Moves(sems)
    for target, begin in ((near, (1 - odd) * start), (far, odd * start)):
        rows = pl.ds(pl.multiple_of(begin, LANES), margin)
        moves.begin(inner.at[:, rows, :], target.at[:, :, pl.ds(0, LANES)])
        moves.begin(outer.at[:, rows, :], target.at[:, :, pl.ds(LANES, LANES)])
    moves.wait()


def corners(inner, outer):
    shape = (2, inner.shape[2], 2 * LANES)
    return pl.pallas_call(
        corners_kernel,
        out_shape=shapes(shape, shape),
        in_specs=[FREE] * 2,
        out_specs=[FREE] * 2,
        scratch_shapes=[pltpu.SemaphoreType.DMA((4,))],
        compiler_params=pltpu.CompilerParams(vmem_limit_bytes=MIB),
        cost_estimate=pl.CostEstimate(flops=0, bytes_accessed=MIB, transcendentals=0),
        name="corners",
    )(inner, outer)


def add_sides(add, inner, outer, last):
    core = lax.axis_index(CORE)

    @pl.when(core == 0)
    def _():
        add(outer, 0)
        add(inner, last)

    @pl.when(core != 0)
    def _():
        add(inner, 0)
        add(outer, last)


def turn_kernel(
    pieces_in, grown, inner_in, outer_in, copies_out, near_out, far_out,
    pieces, strips, inner, outer, sems, out_sems,
):
    margin, cols = strips.shape[2:]
    rows = inner_in.shape[1] - 2 * margin
    low, high = pl.ds(0, margin), pl.ds(margin + rows, margin)
    center = pl.ds(LANES, cols)
    first = Moves(sems)
    first.begin(pieces_in, pieces)
    for side_in, side in ((inner_in, inner), (outer_in, outer)):
        first.begin(side_in.at[:, low, :], side.at[:, low, :])
        first.begin(side_in.at[:, high, :], side.at[:, pl.ds(margin, margin), :])
    first.begin(grown.at[:, low, center], strips.at[0])
    first.begin(grown.at[:, high, center], strips.at[1])
    first.wait()
    last = Moves(out_sems)

    def add(side, start):
        lanes = pl.ds(start, LANES)
        strips[0, :, :, lanes] += side[:, :margin, :]
        strips[1, :, :, lanes] += side[:, margin:, :]

    add_sides(add, inner, outer, cols - LANES)
    odd = odd_row()
    last.begin(strips.at[1 - odd], near_out)
    last.begin(strips.at[odd], far_out)
    total = pieces[0]
    for n in range(1, pieces.shape[0]):
        total = total + pieces[n]
    for n in range(pieces.shape[0]):
        pieces[n] = total
    last.begin(pieces, copies_out)
    last.wait()


def turn(pieces, grown, inner, outer):
    margin = inner.shape[2]
    strip, ends = (2, margin, grown.shape[2] - 2 * LANES), (2, 2 * margin, margin)
    return pl.pallas_call(
        turn_kernel,
        out_shape=shapes(pieces.shape, strip, strip),
        in_specs=[FREE] * 4,
        out_specs=[FREE] * 3,
        scratch_shapes=[pltpu.VMEM(x, F32) for x in (pieces.shape, (2,) + strip, ends, ends)]
        + [pltpu.SemaphoreType.DMA((7,)), pltpu.SemaphoreType.DMA((3,))],
        compiler_params=pltpu.CompilerParams(vmem_limit_bytes=8 * MIB),
        cost_estimate=pl.CostEstimate(flops=600_000, bytes_accessed=7 * MIB, transcendentals=0),
        name="turn",
    )(pieces, grown, inner, outer)


def finish_kernel(grown, inner_in, outer_in, near, far, out, center, inner, outer, strips, sems):
    margin = near.shape[1]
    rows, cols = center.shape[1:]
    middle = pl.ds(margin, rows)
    odd = odd_row()
    loads = Moves(sems)
    loads.begin(grown.at[:, middle, pl.ds(LANES, cols)], center)
    loads.begin(inner_in.at[:, middle], inner)
    loads.begin(outer_in.at[:, middle], outer)
    loads.begin(near, strips.at[1 - odd])
    loads.begin(far, strips.at[odd])
    loads.wait()
    moves = Moves(sems)
    for p in range(2):
        center[p, :margin, :] += strips[0, p]
        center[p, rows - margin :, :] += strips[1, p]

        def add(side, start):
            center[p, :, pl.ds(start, LANES)] += side[p]

        add_sides(add, inner, outer, cols - LANES)
        moves.begin(center.at[p], out.at[p])
    moves.wait()


def finish(grown, inner, outer, near, far):
    center = (2, inner.shape[1] - 2 * near.shape[1], near.shape[2])
    side = (2, center[1], LANES)
    made = (center, side, side, (2,) + near.shape)
    return pl.pallas_call(
        finish_kernel,
        out_shape=jax.ShapeDtypeStruct(center, F32),
        in_specs=[FREE] * 5,
        out_specs=FREE,
        scratch_shapes=[pltpu.VMEM(x, F32) for x in made] + [pltpu.SemaphoreType.DMA((5,))],
        compiler_params=pltpu.CompilerParams(vmem_limit_bytes=8 * MIB),
        cost_estimate=pl.CostEstimate(flops=600_000, bytes_accessed=7 * MIB, transcendentals=0),
        name="finish",
    )(grown, inner, outer, near, far)


def join_kernel(own, other, out, sems):
    core = lax.axis_index(CORE)
    moves = Moves(sems)
    moves.begin(own, out.at[core])
    moves.begin(other, out.at[1 - core])
    moves.wait()


def join(own, other):
    return pl.pallas_call(
        join_kernel,
        out_shape=jax.ShapeDtypeStruct((2,) + own.shape, F32),
        in_specs=[FREE, FREE],
        out_specs=FREE,
        scratch_shapes=[pltpu.SemaphoreType.DMA((2,))],
        compiler_params=pltpu.CompilerParams(vmem_limit_bytes=MIB),
        cost_estimate=pl.CostEstimate(flops=0, bytes_accessed=4 * MIB, transcendentals=0),
        name="join",
    )(own, other)


def swap_inner(block, axes):
    count = lax.axis_size(axes)
    return lax.ppermute(block, axes, [(i, i ^ 1) for i in range(count)])


def swap_outer(block, axes):
    count = lax.axis_size(axes)
    pairs = [(i, i + 1) for i in range(1, count - 1, 2)]
    return lax.ppermute(block, axes, pairs + [(j, i) for i, j in pairs])


def exchange(counts, pieces):
    def send(given):
        return lax.all_to_all(given, CHIP, 0, 0, tiled=True)

    return lax.cond(counts[0, 0] > 0, send, jnp.zeros_like, pieces)


def on_device(object_field, probe, patterns, offsets, counts):
    width = patterns.shape[1]
    modes = probe.shape[1]

    near, far, inner, outer = cut(object_field, width // 2)
    near = swap_inner(near, ROW)
    far = swap_outer(far, ROW)
    outer = swap_outer(outer, COL)
    inner = swap_inner(inner, COL)
    corner_near, corner_far = corners(inner, outer)
    corner_near = swap_inner(corner_near, ROW)
    corner_far = swap_outer(corner_far, ROW)

    table = jnp.asarray(tables(width))
    measured, wide = prepare(patterns, probe)
    ext, totals, keep, send = first_slots(
        offsets, counts, object_field, inner, outer, measured, wide, table
    )
    sides = (near, far, corner_near, corner_far)
    totals, keep, send, inner, outer = second_slots(
        offsets, counts, sides, ext, totals, keep, send, measured, wide, table
    )

    received = swap_inner(send, COL)
    outer = swap_outer(outer, COL)
    inner = swap_inner(inner, COL)
    grown = stash(totals)
    received, grown = lax.optimization_barrier((received, grown))
    pair = pair_sum(keep, received)
    chips = lax.axis_size(CHIP)
    pieces = exchange(counts, pair.reshape(chips, modes * width // chips, width))
    pieces, inner, outer = lax.optimization_barrier((pieces, inner, outer))
    copies, near, far = turn(pieces, grown, inner, outer)
    near = swap_inner(near, ROW)
    far = swap_outer(far, ROW)
    gathered = exchange(counts, copies).reshape(modes, width, width)
    gathered, near, far = lax.optimization_barrier((gathered, near, far))
    other = swap_inner(gathered, COL)
    object_grad = finish(grown, inner, outer, near, far)
    return (object_grad, join(gathered, other))


def solution(mesh):
    rows, cols = mesh.devices.shape
    side = math.isqrt(rows)
    fine = Mesh(mesh.devices.reshape(side, side, cols // 2, 2), CHIP + (CORE,))
    in_specs = (P(None, ROW, COL), P(), P(ROW + COL, None, None), P(None, ROW + COL), P(ROW, COL))
    out_specs = (P(None, ROW, COL), P())
    return jax.shard_map(
        on_device, mesh=fine, in_specs=in_specs, out_specs=out_specs, check_vma=False
    )
```

```python
import math

import jax
import jax.numpy as jnp
import numpy as np
from jax import lax
from jax.experimental import pallas as pl
from jax.experimental.pallas import tpu as pltpu
from jax.sharding import Mesh, PartitionSpec as P

LANES = 128
CHUNK = 32
F32 = jnp.float32
BF16 = jnp.bfloat16
RIGHT = (0, 2)
LEFT = (1, 3)
MIB = 1024 * 1024
SPARE = 23
FREE = pl.BlockSpec(memory_space=pl.ANY)
VMEM = pl.BlockSpec(memory_space=pltpu.VMEM)
ROW, COL, CORE = ("x", "y"), ("z", "core"), "core"
CHIP = ("x", "y", "z")
SMEM = pl.BlockSpec(memory_space=pltpu.SMEM)


def tables(length):
    index = np.arange(length // 2)
    parts = []
    for parity in range(2):
        product = index[:, None] * (2 * index[None, :] + parity) % length
        angle = product * (2.0 * math.pi / length)
        factor = 1.0 / math.sqrt(length)
        re = (np.cos(angle) * factor).astype(BF16)
        im = (-np.sin(angle) * factor).astype(BF16)
        right = np.block([[re, im], [-im, re]])
        parts += [right, right.T]
    return np.stack(parts).astype(BF16)


def dot(a, b):
    return jnp.dot(a, b, preferred_element_type=F32)


def one_slot(number, row, col, ext, pat, probe, table, totals, keep, send, work):
    obj, psi, half, field = work
    width = pat.shape[1]
    modes = probe.shape[1]
    mid = width // 2
    blocks = ext.shape[1] - 2
    core = lax.axis_index(CORE)
    block = jnp.minimum(col // LANES, blocks - 1)
    rest = col - block * LANES
    back_shift = lax.rem(LANES - rest, LANES)
    shift = lax.rem(rest, LANES)
    lane = lax.broadcasted_iota(jnp.int32, (CHUNK, LANES), 1)
    from_first = lane < LANES - rest
    at_or_after = lane >= rest
    turn = (core + jnp.zeros((CHUNK, LANES), jnp.int32)) == 0
    low, high = pl.ds(0, mid), pl.ds(mid, mid)

    def span(c, base=0):
        return pl.ds(base + c * CHUNK, CHUNK)

    def gather_patch():
        for c in range(width // CHUNK):
            source = pl.ds(row + c * CHUNK, CHUNK)
            patch = []
            for p in range(2):
                parts = [
                    pltpu.roll(ext[p, block + j, source, :], back_shift, 1) for j in range(3)
                ]
                patch.append(
                    [
                        jnp.where(from_first, parts[0], parts[1]),
                        jnp.where(from_first, parts[1], parts[2]),
                    ]
                )
            for side, lanes in enumerate((low, high)):
                re, im = patch[0][side], patch[1][side]
                obj[0, span(c), lanes] = jnp.where(turn, re, -im)
                obj[1, span(c), lanes] = jnp.where(turn, im, re)
            for k in range(modes):
                waves = []
                for side, lanes in enumerate((low, high)):
                    o_re, o_im = patch[0][side], patch[1][side]
                    p_re, p_im = probe[0, k, span(c), lanes], probe[1, k, span(c), lanes]
                    waves.append((p_re * o_re - p_im * o_im, p_re * o_im + p_im * o_re))
                for part, lanes in enumerate((low, high)):
                    a, b = waves[0][part], waves[1][part]
                    psi[k, 0, span(c), lanes] = (a + b).astype(BF16)
                    psi[k, 1, span(c), lanes] = (a - b).astype(BF16)

    def right_forward_all():
        for parity, lanes in enumerate((low, high)):
            whole = dot(psi[:, parity].reshape(modes * width, width), table[RIGHT[parity]])
            for k in range(modes):
                right_forward(k, lanes, whole[k * width : (k + 1) * width])

    def right_forward(k, lanes, y):
        top, bottom = y[:mid], y[mid:]
        total, difference = (top + bottom).astype(BF16), (top - bottom).astype(BF16)
        half[k, 0, low, lanes] = total[:, :mid]
        half[k, 0, high, lanes] = total[:, mid:]
        half[k, 1, low, lanes] = difference[:, :mid]
        half[k, 1, high, lanes] = difference[:, mid:]

    def left_forward(k):
        for parity in range(2):
            field[k, parity] = dot(table[LEFT[parity]], half[k, parity])

    def make_all_chi():
        for parity in range(2):
            for c in range(mid // CHUNK):
                values = [
                    (field[k, parity, span(c), :], field[k, parity, span(c, mid), :])
                    for k in range(modes)
                ]
                total = None
                for re, im in values:
                    square = re * re + im * im
                    total = square if total is None else total + square
                measured = pat[number, span(c, parity * mid), :]
                scale = 1.0 - measured * lax.rsqrt(jnp.maximum(total, 1.0))
                rows = span(c, parity * mid)
                for k, (re, im) in enumerate(values):
                    re, im = (re * scale).astype(BF16), (im * scale).astype(BF16)
                    psi[k, 0, rows, low] = re[:, :mid]
                    psi[k, 0, rows, high] = im[:, :mid]
                    psi[k, 1, rows, low] = re[:, mid:]
                    psi[k, 1, rows, high] = im[:, mid:]

    def right_backward_all():
        evens = dot(psi[:, 0].reshape(modes * width, width), table[LEFT[0]])
        odds = dot(psi[:, 1].reshape(modes * width, width), table[LEFT[1]])
        for k in range(modes):
            right_backward(k, evens[k * width : (k + 1) * width], odds[k * width : (k + 1) * width])

    def right_backward(k, even, odd):
        for value, lanes in (((even + odd).astype(BF16), low), ((even - odd).astype(BF16), high)):
            for parity in range(2):
                rows = value[parity * mid : parity * mid + mid]
                half[k, parity, low, lanes] = rows[:, :mid]
                half[k, parity, high, lanes] = rows[:, mid:]

    def left_backward(k):
        for parity in range(2):
            field[k, parity] = dot(table[RIGHT[parity]], half[k, parity])

    def collect_all():
        for c in range(mid // CHUNK):
            for top in range(2):
                rows = span(c, top * mid)
                target = pl.ds(row + top * mid + c * CHUNK, CHUNK)
                o_re, o_im = obj[0, rows, :], obj[1, rows, :]
                sums = [None, None]
                for k in range(modes):
                    even_re, odd_re = field[k, 0, span(c), :], field[k, 1, span(c), :]
                    even_im, odd_im = field[k, 0, span(c, mid), :], field[k, 1, span(c, mid), :]
                    re = even_re - odd_re if top else even_re + odd_re
                    im = even_im - odd_im if top else even_im + odd_im
                    p_re, p_im = probe[0, k, rows, :], probe[1, k, rows, :]
                    adds = (p_re * re + p_im * im, p_re * im - p_im * re)
                    sums = [x if k == 0 else t + x for t, x in zip(sums, adds)]
                    keep[k, rows, :] += o_re * re + o_im * im
                    send[k, rows, :] += o_re * im - o_im * re
                for p in range(2):
                    first = pltpu.roll(sums[p][:, :LANES], shift, 1)
                    second = pltpu.roll(sums[p][:, LANES:], shift, 1)
                    totals[p, block, target, :] += jnp.where(at_or_after, first, 0.0)
                    totals[p, block + 1, target, :] += jnp.where(at_or_after, second, first)
                    totals[p, block + 2, target, :] += jnp.where(at_or_after, 0.0, second)

    gather_patch()
    right_forward_all()
    for k in range(modes):
        left_forward(k)
    make_all_chi()
    right_backward_all()
    for k in range(modes):
        left_backward(k)
    collect_all()


class Moves:
    def __init__(self, sems):
        self.sems = sems
        self.started = []

    def begin(self, source, target):
        move = pltpu.make_async_copy(source, target, self.sems.at[len(self.started)])
        move.start()
        self.started.append(move)

    def wait(self):
        for move in self.started:
            move.wait()


def visit_all(later, offsets, counts, tile_rows, tile_cols, ext, pat, *rest):
    width = pat.shape[1]
    margin = width // 2
    base_row = lax.axis_index(ROW) * tile_rows - margin
    base_col = lax.axis_index(COL) * tile_cols - margin

    def visit(number, carry):
        row = offsets[0, number] - base_row
        col = offsets[1, number] - base_col
        beyond = jnp.logical_or(row < margin, row + width > margin + tile_rows)

        @pl.when(beyond if later else jnp.logical_not(beyond))
        def _():
            one_slot(number, row, col, ext, pat, *rest)

        return carry

    lax.fori_loop(0, counts[0, 0], visit, 0)


def first_kernel(
    offsets, counts, tile, inner, outer, pat, probe, table,
    ext, totals, keep, send, obj, psi, half, field, sems,
):
    rows, cols = tile.shape[1:]
    margin = inner.shape[2]
    last = cols // LANES + 1
    core = lax.axis_index(CORE)
    middle = pl.ds(margin, rows)
    moves = Moves(sems)
    for j in range(1, last):
        moves.begin(tile.at[:, :, pl.ds((j - 1) * LANES, LANES)], ext.at[:, j, middle, :])
    moves.begin(inner, ext.at[:, (1 - core) * last, middle, :])
    moves.begin(outer, ext.at[:, core * last, middle, :])
    totals[...] = jnp.zeros_like(totals)
    keep[...] = jnp.zeros_like(keep)
    send[...] = jnp.zeros_like(send)
    moves.wait()
    work = (obj, psi, half, field)
    visit_all(False, offsets, counts, rows, cols, ext, pat, probe, table, totals, keep, send, work)


def second_kernel(
    offsets, counts, near, far, corner_near, corner_far, ext_in, totals_in, keep_in,
    send_in, pat, probe, table,
    totals, keep, send, inner_out, outer_out,
    ext, obj, psi, half, field, sems,
):
    margin, cols = near.shape[1:]
    last = ext.shape[1] - 1
    rows = ext.shape[2] - 2 * margin
    core = lax.axis_index(CORE)
    inner_block, outer_block = (1 - core) * last, core * last
    middle = pl.ds(margin, rows)
    moves = Moves(sems)
    moves.begin(ext_in.at[:, :, middle, :], ext.at[:, :, middle, :])
    odd = odd_row()
    near_rows, far_rows = (
        pl.ds(pl.multiple_of(start, LANES), margin)
        for start in ((1 - odd) * (margin + rows), odd * (margin + rows))
    )
    for j in range(1, last):
        lanes = pl.ds((j - 1) * LANES, LANES)
        moves.begin(near.at[:, :, lanes], ext.at[:, j, near_rows, :])
        moves.begin(far.at[:, :, lanes], ext.at[:, j, far_rows, :])
    for n, j in enumerate((inner_block, outer_block)):
        lanes = pl.ds(n * margin, margin)
        moves.begin(corner_near.at[:, :, lanes], ext.at[:, j, near_rows, :])
        moves.begin(corner_far.at[:, :, lanes], ext.at[:, j, far_rows, :])
    totals[...] = totals_in[...]
    keep[...] = keep_in[...]
    send[...] = send_in[...]
    moves.wait()
    work = (obj, psi, half, field)
    visit_all(True, offsets, counts, rows, cols, ext, pat, probe, table, totals, keep, send, work)
    moves = Moves(sems)
    moves.begin(totals.at[:, outer_block], outer_out)
    moves.begin(totals.at[:, inner_block], inner_out)
    moves.wait()


def slot_scratch(modes, width):
    return [
        pltpu.VMEM((2, width, width), F32),
        pltpu.VMEM((modes, 2, width, width), BF16),
        pltpu.VMEM((modes, 2, width, width), BF16),
        pltpu.VMEM((modes, 2, width, width), F32),
        pltpu.SemaphoreType.DMA((16,)),
    ]


def shapes(*dims):
    return [jax.ShapeDtypeStruct(shape, F32) for shape in dims]


def cost(slots, modes, width):
    return pl.CostEstimate(
        flops=slots * modes * width * width * width * 16,
        bytes_accessed=30 * MIB,
        transcendentals=slots * width * width,
    )


def first_slots(offsets, counts, tile, inner, outer, patterns, probe, table):
    modes, width = probe.shape[1:3]
    rows, cols = tile.shape[1:]
    grown = (2, cols // LANES + 2, rows + 2 * inner.shape[2], LANES)
    plane = (modes, width, width)
    return pl.pallas_call(
        first_kernel,
        out_shape=shapes(grown, grown, plane, plane),
        in_specs=[SMEM] * 2 + [FREE] * 3 + [VMEM] * 3,
        out_specs=[VMEM] * 4,
        scratch_shapes=slot_scratch(modes, width),
        compiler_params=pltpu.CompilerParams(vmem_limit_bytes=24 * MIB),
        cost_estimate=cost(4, modes, width),
        name="slots_first",
    )(offsets, counts, tile, inner, outer, patterns, probe, table)


def second_slots(offsets, counts, sides, ext, totals, keep, send, patterns, probe, table):
    modes, width = probe.shape[1:3]
    margin = sides[0].shape[1]
    side = (2, ext.shape[2], LANES)
    return pl.pallas_call(
        second_kernel,
        out_shape=shapes(totals.shape, keep.shape, send.shape, side, side),
        in_specs=[SMEM] * 2 + [FREE] * 5 + [VMEM] * 6,
        out_specs=[VMEM] * 3 + [FREE] * 2,
        scratch_shapes=[pltpu.VMEM(ext.shape, F32)] + slot_scratch(modes, width),
        input_output_aliases={7: 0, 8: 1, 9: 2},
        compiler_params=pltpu.CompilerParams(vmem_limit_bytes=24 * MIB),
        cost_estimate=cost(4, modes, width),
        name="slots_second",
    )(offsets, counts, *sides, ext, totals, keep, send, patterns, probe, table)


def prepare_kernel(patterns, probe, out, wide, moving):
    wide[...] = probe[...].astype(F32)
    slots, width = patterns.shape[:2]
    mid = width // 2
    source = lax.broadcasted_iota(jnp.int32, (width, width), 0)
    target = lax.broadcasted_iota(jnp.int32, (width, width), 1)
    wanted = jnp.where(target < mid, 2 * target, 2 * target - (width - 1))
    pick = (source == wanted).astype(BF16)

    def one(number, carry):
        value = patterns[number]
        total = None
        for _ in range(2):
            part = value.astype(BF16)
            value = value - part.astype(F32)
            moved = dot(part, pick)
            total = moved if total is None else total + moved
        for side in range(2):
            lanes = pl.ds(side * mid, mid)
            moving[side] = total[:, side * mid : side * mid + mid]
            for parity in range(2):
                out[number, pl.ds(parity * mid, mid), lanes] = moving[side, pl.ds(parity, mid, 2), :]
        return carry

    lax.fori_loop(0, slots, one, 0)


def prepare(patterns, probe):
    return pl.pallas_call(
        prepare_kernel,
        out_shape=shapes(patterns.shape, probe.shape),
        in_specs=[VMEM] * 2,
        out_specs=[VMEM] * 2,
        scratch_shapes=[pltpu.VMEM((2, patterns.shape[1], patterns.shape[2] // 2), F32)],
        compiler_params=pltpu.CompilerParams(vmem_limit_bytes=12 * MIB),
        cost_estimate=pl.CostEstimate(
            flops=patterns.size * 256 * 6, bytes_accessed=9 * MIB, transcendentals=0
        ),
        name="prepare",
    )(patterns, probe)


def odd_row():
    return lax.rem(lax.axis_index(ROW), 2)


def cut_kernel(tile, near, far, inner, outer, sems):
    margin = near.shape[1]
    rows, cols = tile.shape[1:]
    core = lax.axis_index(CORE)
    odd = odd_row()

    def band(start):
        return tile.at[:, pl.ds(pl.multiple_of(start, LANES), margin), :]

    def strip(start):
        return tile.at[:, :, pl.ds(pl.multiple_of(start, LANES), margin)]

    moves = Moves(sems)
    moves.begin(band((1 - odd) * (rows - margin)), near)
    moves.begin(band(odd * (rows - margin)), far)
    moves.begin(strip(core * (cols - margin)), outer)
    moves.begin(strip((1 - core) * (cols - margin)), inner)
    moves.wait()


def cut(tile, margin):
    rows, cols = tile.shape[1:]
    return pl.pallas_call(
        cut_kernel,
        out_shape=shapes((2, margin, cols), (2, margin, cols), (2, rows, margin), (2, rows, margin)),
        in_specs=[FREE],
        out_specs=[FREE] * 4,
        scratch_shapes=[pltpu.SemaphoreType.DMA((4,))],
        compiler_params=pltpu.CompilerParams(vmem_limit_bytes=MIB),
        cost_estimate=pl.CostEstimate(flops=0, bytes_accessed=4 * MIB, transcendentals=0),
        name="cut",
    )(tile)


def pair_kernel(keep, received, out, total, sems):
    sign = jnp.where(lax.axis_index(CORE) == 0, -1.0, 1.0).astype(F32)
    moves = Moves(sems)
    for k in range(keep.shape[0]):
        total[k] = keep[k] + received[k] * sign
        moves.begin(total.at[k], out.at[k])
    moves.wait()


def pair_sum(keep, received):
    return pl.pallas_call(
        pair_kernel,
        out_shape=jax.ShapeDtypeStruct(keep.shape, F32),
        in_specs=[VMEM] * 2,
        out_specs=FREE,
        scratch_shapes=[pltpu.VMEM(keep.shape, F32), pltpu.SemaphoreType.DMA((keep.shape[0],))],
        compiler_params=pltpu.CompilerParams(vmem_limit_bytes=8 * MIB),
        cost_estimate=pl.CostEstimate(flops=600_000, bytes_accessed=3 * MIB, transcendentals=0),
        name="pair_sum",
    )(keep, received)


def stash_kernel(totals, out, sems):
    rows = pl.ds(0, totals.shape[2])
    moves = Moves(sems)
    for j in range(totals.shape[1] - 2):
        moves.begin(totals.at[:, 1 + j], out.at[:, rows, pl.ds(j * LANES, LANES)])
    moves.wait()


def stash(totals):
    planes, blocks, rows, lanes = totals.shape
    return pl.pallas_call(
        stash_kernel,
        out_shape=jax.ShapeDtypeStruct((planes, SPARE * rows, (blocks - 2) * lanes), F32),
        in_specs=[VMEM],
        out_specs=FREE,
        scratch_shapes=[pltpu.SemaphoreType.DMA((blocks,))],
        compiler_params=pltpu.CompilerParams(vmem_limit_bytes=6 * MIB),
        cost_estimate=pl.CostEstimate(flops=0, bytes_accessed=6 * MIB, transcendentals=0),
        name="stash",
    )(totals)


def corners_kernel(inner, outer, near, far, sems):
    margin = near.shape[1]
    start = inner.shape[1] - margin
    odd = odd_row()
    moves = Moves(sems)
    for target, begin in ((near, (1 - odd) * start), (far, odd * start)):
        rows = pl.ds(pl.multiple_of(begin, LANES), margin)
        moves.begin(inner.at[:, rows, :], target.at[:, :, pl.ds(0, LANES)])
        moves.begin(outer.at[:, rows, :], target.at[:, :, pl.ds(LANES, LANES)])
    moves.wait()


def corners(inner, outer):
    shape = (2, inner.shape[2], 2 * LANES)
    return pl.pallas_call(
        corners_kernel,
        out_shape=shapes(shape, shape),
        in_specs=[FREE] * 2,
        out_specs=[FREE] * 2,
        scratch_shapes=[pltpu.SemaphoreType.DMA((4,))],
        compiler_params=pltpu.CompilerParams(vmem_limit_bytes=MIB),
        cost_estimate=pl.CostEstimate(flops=0, bytes_accessed=MIB, transcendentals=0),
        name="corners",
    )(inner, outer)


def add_sides(add, inner, outer, last):
    core = lax.axis_index(CORE)

    @pl.when(core == 0)
    def _():
        add(outer, 0)
        add(inner, last)

    @pl.when(core != 0)
    def _():
        add(inner, 0)
        add(outer, last)


def spread_kernel(grown, inner_in, outer_in, near_out, far_out, strips, inner, outer, sems):
    margin, cols = strips.shape[2:]
    low, high = pl.ds(0, margin), pl.ds(inner_in.shape[1] - margin, margin)
    first = Moves(sems)
    for side_in, side in ((inner_in, inner), (outer_in, outer)):
        first.begin(side_in.at[:, low, :], side.at[:, low, :])
        first.begin(side_in.at[:, high, :], side.at[:, pl.ds(margin, margin), :])
    first.begin(grown.at[:, low, :], strips.at[0])
    first.begin(grown.at[:, high, :], strips.at[1])
    first.wait()
    last = Moves(sems)

    def add(side, start):
        lanes = pl.ds(start, LANES)
        strips[0, :, :, lanes] += side[:, :margin, :]
        strips[1, :, :, lanes] += side[:, margin:, :]

    add_sides(add, inner, outer, cols - LANES)
    odd = odd_row()
    last.begin(strips.at[1 - odd], near_out)
    last.begin(strips.at[odd], far_out)
    last.wait()


def spread(grown, inner, outer):
    margin = inner.shape[2]
    strip, ends = (2, margin, grown.shape[2]), (2, 2 * margin, margin)
    return pl.pallas_call(
        spread_kernel,
        out_shape=shapes(strip, strip),
        in_specs=[FREE] * 3,
        out_specs=[FREE] * 2,
        scratch_shapes=[pltpu.VMEM(x, F32) for x in ((2,) + strip, ends, ends)]
        + [pltpu.SemaphoreType.DMA((6,))],
        compiler_params=pltpu.CompilerParams(vmem_limit_bytes=6 * MIB),
        cost_estimate=pl.CostEstimate(flops=600_000, bytes_accessed=4 * MIB, transcendentals=0),
        name="spread",
    )(grown, inner, outer)


def fold_kernel(pieces, copies_out, copies, sems):
    count = pieces.shape[0]
    total = pieces[0]
    for n in range(1, count):
        total = total + pieces[n]
    moves = Moves(sems)
    part = count // 4
    for q in range(4):
        for n in range(part):
            copies[q * part + n] = total
        span = pl.ds(q * part, part)
        moves.begin(copies.at[span], copies_out.at[span])
    moves.wait()


def fold(pieces):
    return pl.pallas_call(
        fold_kernel,
        out_shape=jax.ShapeDtypeStruct(pieces.shape, F32),
        in_specs=[VMEM],
        out_specs=FREE,
        scratch_shapes=[pltpu.VMEM(pieces.shape, F32), pltpu.SemaphoreType.DMA((4,))],
        compiler_params=pltpu.CompilerParams(vmem_limit_bytes=4 * MIB),
        cost_estimate=pl.CostEstimate(flops=300_000, bytes_accessed=2 * MIB, transcendentals=0),
        name="fold",
    )(pieces)


def finish_kernel(grown, inner_in, outer_in, near, far, out, center, inner, outer, strips, sems):
    margin = near.shape[1]
    rows, cols = center.shape[1:]
    middle = pl.ds(margin, rows)
    odd = odd_row()
    loads = []
    for p in range(2):
        moves = Moves(sems.at[p])
        moves.begin(grown.at[p, middle, :], center.at[p])
        moves.begin(inner_in.at[p, middle], inner.at[p])
        moves.begin(outer_in.at[p, middle], outer.at[p])
        moves.begin(near.at[p], strips.at[1 - odd, p])
        moves.begin(far.at[p], strips.at[odd, p])
        loads.append(moves)
    stores = Moves(sems.at[2])
    for p in range(2):
        loads[p].wait()
        center[p, :margin, :] += strips[0, p]
        center[p, rows - margin :, :] += strips[1, p]

        def add(side, start):
            center[p, :, pl.ds(start, LANES)] += side[p]

        add_sides(add, inner, outer, cols - LANES)
        stores.begin(center.at[p], out.at[p])
    stores.wait()


def finish(grown, inner, outer, near, far):
    center = (2, inner.shape[1] - 2 * near.shape[1], near.shape[2])
    side = (2, center[1], LANES)
    made = (center, side, side, (2,) + near.shape)
    return pl.pallas_call(
        finish_kernel,
        out_shape=jax.ShapeDtypeStruct(center, F32),
        in_specs=[FREE] * 5,
        out_specs=FREE,
        scratch_shapes=[pltpu.VMEM(x, F32) for x in made] + [pltpu.SemaphoreType.DMA((3, 5))],
        compiler_params=pltpu.CompilerParams(vmem_limit_bytes=8 * MIB),
        cost_estimate=pl.CostEstimate(flops=600_000, bytes_accessed=7 * MIB, transcendentals=0),
        name="finish",
    )(grown, inner, outer, near, far)


def join_kernel(own, other, out, sems):
    core = lax.axis_index(CORE)
    moves = Moves(sems)
    moves.begin(own, out.at[core])
    moves.begin(other, out.at[1 - core])
    moves.wait()


def join(own, other):
    return pl.pallas_call(
        join_kernel,
        out_shape=jax.ShapeDtypeStruct((2,) + own.shape, F32),
        in_specs=[FREE, FREE],
        out_specs=FREE,
        scratch_shapes=[pltpu.SemaphoreType.DMA((2,))],
        compiler_params=pltpu.CompilerParams(vmem_limit_bytes=MIB),
        cost_estimate=pl.CostEstimate(flops=0, bytes_accessed=4 * MIB, transcendentals=0),
        name="join",
    )(own, other)


def swap_inner(block, axes):
    count = lax.axis_size(axes)
    return lax.ppermute(block, axes, [(i, i ^ 1) for i in range(count)])


def swap_outer(block, axes):
    count = lax.axis_size(axes)
    pairs = [(i, i + 1) for i in range(1, count - 1, 2)]
    return lax.ppermute(block, axes, pairs + [(j, i) for i, j in pairs])


def exchange(counts, pieces):
    def send(given):
        return lax.all_to_all(given, CHIP, 0, 0, tiled=True)

    return lax.cond(counts[0, 0] > 0, send, jnp.zeros_like, pieces)


def on_device(object_field, probe, patterns, offsets, counts):
    width = patterns.shape[1]
    modes = probe.shape[1]

    near, far, inner, outer = cut(object_field, width // 2)
    near = swap_inner(near, ROW)
    far = swap_outer(far, ROW)
    outer = swap_outer(outer, COL)
    inner = swap_inner(inner, COL)
    corner_near, corner_far = corners(inner, outer)
    corner_near = swap_inner(corner_near, ROW)
    corner_far = swap_outer(corner_far, ROW)

    table = jnp.asarray(tables(width))
    measured, wide = prepare(patterns, probe)
    ext, totals, keep, send = first_slots(
        offsets, counts, object_field, inner, outer, measured, wide, table
    )
    sides = (near, far, corner_near, corner_far)
    totals, keep, send, inner, outer = second_slots(
        offsets, counts, sides, ext, totals, keep, send, measured, wide, table
    )

    received = swap_inner(send, COL)
    outer = swap_outer(outer, COL)
    inner = swap_inner(inner, COL)
    grown = stash(totals)
    received, grown = lax.optimization_barrier((received, grown))
    pair = pair_sum(keep, received)
    chips = lax.axis_size(CHIP)
    pieces = exchange(counts, pair.reshape(chips, modes * width // chips, width))
    pieces, inner, outer = lax.optimization_barrier((pieces, inner, outer))
    near, far = spread(grown, inner, outer)
    pieces, near, far = lax.optimization_barrier((pieces, near, far))
    near = swap_inner(near, ROW)
    far = swap_outer(far, ROW)
    gathered = exchange(counts, fold(pieces)).reshape(modes, width, width)
    gathered, near, far = lax.optimization_barrier((gathered, near, far))
    other = swap_inner(gathered, COL)
    object_grad = finish(grown, inner, outer, near, far)
    return (object_grad, join(gathered, other))


def solution(mesh):
    rows, cols = mesh.devices.shape
    side = math.isqrt(rows)
    fine = Mesh(mesh.devices.reshape(side, side, cols // 2, 2), CHIP + (CORE,))
    in_specs = (P(None, ROW, COL), P(), P(ROW + COL, None, None), P(None, ROW + COL), P(ROW, COL))
    out_specs = (P(None, ROW, COL), P())
    return jax.shard_map(
        on_device, mesh=fine, in_specs=in_specs, out_specs=out_specs, check_vma=False
    )
```

```python
import math

import jax
import jax.numpy as jnp
import numpy as np
from jax import lax
from jax.experimental import pallas as pl
from jax.experimental.pallas import tpu as pltpu
from jax.sharding import Mesh, PartitionSpec as P

LANES = 128
CHUNK = 32
F32 = jnp.float32
BF16 = jnp.bfloat16
RIGHT = (0, 2)
LEFT = (1, 3)
MIB = 1024 * 1024
SPARE = 23
FREE = pl.BlockSpec(memory_space=pl.ANY)
VMEM = pl.BlockSpec(memory_space=pltpu.VMEM)
ROW, COL, CORE = ("x", "y"), ("z", "core"), "core"
CHIP = ("x", "y", "z")
SMEM = pl.BlockSpec(memory_space=pltpu.SMEM)


def tables(length):
    index = np.arange(length // 2)
    parts = []
    for parity in range(2):
        product = index[:, None] * (2 * index[None, :] + parity) % length
        angle = product * (2.0 * math.pi / length)
        factor = 1.0 / math.sqrt(length)
        re = (np.cos(angle) * factor).astype(BF16)
        im = (-np.sin(angle) * factor).astype(BF16)
        right = np.block([[re, im], [-im, re]])
        parts += [right, right.T]
    return np.stack(parts).astype(BF16)


def dot(a, b):
    return jnp.dot(a, b, preferred_element_type=F32)


def one_slot(number, row, col, ext, pat, probe, table, totals, keep, send, work):
    obj, psi, half, field = work
    width = pat.shape[1]
    modes = probe.shape[1]
    mid = width // 2
    blocks = ext.shape[1] - 2
    core = lax.axis_index(CORE)
    block = jnp.minimum(col // LANES, blocks - 1)
    rest = col - block * LANES
    back_shift = lax.rem(LANES - rest, LANES)
    shift = lax.rem(rest, LANES)
    lane = lax.broadcasted_iota(jnp.int32, (CHUNK, LANES), 1)
    from_first = lane < LANES - rest
    at_or_after = lane >= rest
    turn = (core + jnp.zeros((CHUNK, LANES), jnp.int32)) == 0
    low, high = pl.ds(0, mid), pl.ds(mid, mid)

    def span(c, base=0):
        return pl.ds(base + c * CHUNK, CHUNK)

    def gather_patch():
        for c in range(width // CHUNK):
            source = pl.ds(row + c * CHUNK, CHUNK)
            patch = []
            for p in range(2):
                parts = [
                    pltpu.roll(ext[p, block + j, source, :], back_shift, 1) for j in range(3)
                ]
                patch.append(
                    [
                        jnp.where(from_first, parts[0], parts[1]),
                        jnp.where(from_first, parts[1], parts[2]),
                    ]
                )
            for side, lanes in enumerate((low, high)):
                re, im = patch[0][side], patch[1][side]
                obj[0, span(c), lanes] = jnp.where(turn, re, -im)
                obj[1, span(c), lanes] = jnp.where(turn, im, re)
            for k in range(modes):
                waves = []
                for side, lanes in enumerate((low, high)):
                    o_re, o_im = patch[0][side], patch[1][side]
                    p_re, p_im = probe[0, k, span(c), lanes], probe[1, k, span(c), lanes]
                    waves.append((p_re * o_re - p_im * o_im, p_re * o_im + p_im * o_re))
                for part, lanes in enumerate((low, high)):
                    a, b = waves[0][part], waves[1][part]
                    psi[k, 0, span(c), lanes] = (a + b).astype(BF16)
                    psi[k, 1, span(c), lanes] = (a - b).astype(BF16)

    def right_forward_all():
        for parity, lanes in enumerate((low, high)):
            whole = dot(psi[:, parity].reshape(modes * width, width), table[RIGHT[parity]])
            for k in range(modes):
                right_forward(k, lanes, whole[k * width : (k + 1) * width])

    def right_forward(k, lanes, y):
        top, bottom = y[:mid], y[mid:]
        total, difference = (top + bottom).astype(BF16), (top - bottom).astype(BF16)
        half[k, 0, low, lanes] = total[:, :mid]
        half[k, 0, high, lanes] = total[:, mid:]
        half[k, 1, low, lanes] = difference[:, :mid]
        half[k, 1, high, lanes] = difference[:, mid:]

    def left_forward(k):
        for parity in range(2):
            field[k, parity] = dot(table[LEFT[parity]], half[k, parity])

    def left_forward_all():
        for k in range(modes):
            left_forward(k)

    def left_backward_all():
        for k in range(modes):
            left_backward(k)

    def make_all_chi():
        for parity in range(2):
            for c in range(mid // CHUNK):
                values = [
                    (field[k, parity, span(c), :], field[k, parity, span(c, mid), :])
                    for k in range(modes)
                ]
                total = None
                for re, im in values:
                    square = re * re + im * im
                    total = square if total is None else total + square
                measured = pat[number, span(c, parity * mid), :]
                scale = 1.0 - measured * lax.rsqrt(jnp.maximum(total, 1.0))
                rows = span(c, parity * mid)
                for k, (re, im) in enumerate(values):
                    re, im = (re * scale).astype(BF16), (im * scale).astype(BF16)
                    psi[k, 0, rows, low] = re[:, :mid]
                    psi[k, 0, rows, high] = im[:, :mid]
                    psi[k, 1, rows, low] = re[:, mid:]
                    psi[k, 1, rows, high] = im[:, mid:]

    def right_backward_all():
        evens = dot(psi[:, 0].reshape(modes * width, width), table[LEFT[0]])
        odds = dot(psi[:, 1].reshape(modes * width, width), table[LEFT[1]])
        for k in range(modes):
            right_backward(k, evens[k * width : (k + 1) * width], odds[k * width : (k + 1) * width])

    def right_backward(k, even, odd):
        for value, lanes in (((even + odd).astype(BF16), low), ((even - odd).astype(BF16), high)):
            for parity in range(2):
                rows = value[parity * mid : parity * mid + mid]
                half[k, parity, low, lanes] = rows[:, :mid]
                half[k, parity, high, lanes] = rows[:, mid:]

    def left_backward(k):
        for parity in range(2):
            field[k, parity] = dot(table[RIGHT[parity]], half[k, parity])

    def collect_all():
        for c in range(mid // CHUNK):
            for top in range(2):
                rows = span(c, top * mid)
                target = pl.ds(row + top * mid + c * CHUNK, CHUNK)
                o_re, o_im = obj[0, rows, :], obj[1, rows, :]
                sums = [None, None]
                for k in range(modes):
                    even_re, odd_re = field[k, 0, span(c), :], field[k, 1, span(c), :]
                    even_im, odd_im = field[k, 0, span(c, mid), :], field[k, 1, span(c, mid), :]
                    re = even_re - odd_re if top else even_re + odd_re
                    im = even_im - odd_im if top else even_im + odd_im
                    p_re, p_im = probe[0, k, rows, :], probe[1, k, rows, :]
                    adds = (p_re * re + p_im * im, p_re * im - p_im * re)
                    sums = [x if k == 0 else t + x for t, x in zip(sums, adds)]
                    keep[k, rows, :] += o_re * re + o_im * im
                    send[k, rows, :] += o_re * im - o_im * re
                for p in range(2):
                    first = pltpu.roll(sums[p][:, :LANES], shift, 1)
                    second = pltpu.roll(sums[p][:, LANES:], shift, 1)
                    totals[p, block, target, :] += jnp.where(at_or_after, first, 0.0)
                    totals[p, block + 1, target, :] += jnp.where(at_or_after, second, first)
                    totals[p, block + 2, target, :] += jnp.where(at_or_after, 0.0, second)

    return (
        gather_patch, right_forward_all, left_forward_all, make_all_chi, right_backward_all,
        left_backward_all, collect_all,
    )


class Moves:
    def __init__(self, sems):
        self.sems = sems
        self.started = []

    def begin(self, source, target):
        move = pltpu.make_async_copy(source, target, self.sems.at[len(self.started)])
        move.start()
        self.started.append(move)

    def wait(self):
        for move in self.started:
            move.wait()


def visit_all(later, offsets, counts, tile_rows, tile_cols, queue, works, ext, pat, *rest):
    width = pat.shape[1]
    margin = width // 2
    base_row = lax.axis_index(ROW) * tile_rows - margin
    base_col = lax.axis_index(COL) * tile_cols - margin

    def enter(number, count):
        row = offsets[0, number] - base_row
        beyond = jnp.logical_or(row < margin, row + width > margin + tile_rows)
        wanted = beyond if later else jnp.logical_not(beyond)

        @pl.when(wanted)
        def _():
            queue[count] = number

        return count + wanted.astype(jnp.int32)

    count = lax.fori_loop(0, counts[0, 0], enter, 0)

    def phases(place, work):
        number = queue[place]
        row, col = offsets[0, number] - base_row, offsets[1, number] - base_col
        return one_slot(number, row, col, ext, pat, *rest, work)

    def two(i, carry):
        for both in zip(phases(2 * i, works[0]), phases(2 * i + 1, works[1])):
            for phase in both:
                phase()
        return carry

    lax.fori_loop(0, count // 2, two, 0)

    @pl.when(lax.rem(count, 2) == 1)
    def _():
        for phase in phases(count - 1, works[0]):
            phase()


def first_kernel(
    offsets, counts, tile, inner, outer, pat, probe, table,
    ext, totals, keep, send, obj, psi, half, field, queue, sems,
):
    rows, cols = tile.shape[1:]
    margin = inner.shape[2]
    last = cols // LANES + 1
    core = lax.axis_index(CORE)
    middle = pl.ds(margin, rows)
    moves = Moves(sems)
    for j in range(1, last):
        moves.begin(tile.at[:, :, pl.ds((j - 1) * LANES, LANES)], ext.at[:, j, middle, :])
    moves.begin(inner, ext.at[:, (1 - core) * last, middle, :])
    moves.begin(outer, ext.at[:, core * last, middle, :])
    totals[...] = jnp.zeros_like(totals)
    keep[...] = jnp.zeros_like(keep)
    send[...] = jnp.zeros_like(send)
    moves.wait()
    works = [tuple(x.at[n] for x in (obj, psi, half, field)) for n in range(2)]
    visit_all(False, offsets, counts, rows, cols, queue, works, ext, pat, probe, table, totals, keep, send)


def second_kernel(
    offsets, counts, near, far, corner_near, corner_far, ext_in, totals_in, keep_in,
    send_in, pat, probe, table,
    totals, keep, send, inner_out, outer_out,
    ext, obj, psi, half, field, queue, sems,
):
    margin, cols = near.shape[1:]
    last = ext.shape[1] - 1
    rows = ext.shape[2] - 2 * margin
    core = lax.axis_index(CORE)
    inner_block, outer_block = (1 - core) * last, core * last
    middle = pl.ds(margin, rows)
    moves = Moves(sems)
    moves.begin(ext_in.at[:, :, middle, :], ext.at[:, :, middle, :])
    odd = odd_row()
    near_rows, far_rows = (
        pl.ds(pl.multiple_of(start, LANES), margin)
        for start in ((1 - odd) * (margin + rows), odd * (margin + rows))
    )
    for j in range(1, last):
        lanes = pl.ds((j - 1) * LANES, LANES)
        moves.begin(near.at[:, :, lanes], ext.at[:, j, near_rows, :])
        moves.begin(far.at[:, :, lanes], ext.at[:, j, far_rows, :])
    for n, j in enumerate((inner_block, outer_block)):
        lanes = pl.ds(n * margin, margin)
        moves.begin(corner_near.at[:, :, lanes], ext.at[:, j, near_rows, :])
        moves.begin(corner_far.at[:, :, lanes], ext.at[:, j, far_rows, :])
    totals[...] = totals_in[...]
    keep[...] = keep_in[...]
    send[...] = send_in[...]
    moves.wait()
    works = [tuple(x.at[n] for x in (obj, psi, half, field)) for n in range(2)]
    visit_all(True, offsets, counts, rows, cols, queue, works, ext, pat, probe, table, totals, keep, send)
    moves = Moves(sems)
    moves.begin(totals.at[:, outer_block], outer_out)
    moves.begin(totals.at[:, inner_block], inner_out)
    moves.wait()


def slot_scratch(modes, width):
    return [
        pltpu.VMEM((2, 2, width, width), F32),
        pltpu.VMEM((2, modes, 2, width, width), BF16),
        pltpu.VMEM((2, modes, 2, width, width), BF16),
        pltpu.VMEM((2, modes, 2, width, width), F32),
        pltpu.SMEM((8,), jnp.int32),
        pltpu.SemaphoreType.DMA((16,)),
    ]


def shapes(*dims):
    return [jax.ShapeDtypeStruct(shape, F32) for shape in dims]


def cost(slots, modes, width):
    return pl.CostEstimate(
        flops=slots * modes * width * width * width * 16,
        bytes_accessed=30 * MIB,
        transcendentals=slots * width * width,
    )


def first_slots(offsets, counts, tile, inner, outer, patterns, probe, table):
    modes, width = probe.shape[1:3]
    rows, cols = tile.shape[1:]
    grown = (2, cols // LANES + 2, rows + 2 * inner.shape[2], LANES)
    plane = (modes, width, width)
    return pl.pallas_call(
        first_kernel,
        out_shape=shapes(grown, grown, plane, plane),
        in_specs=[SMEM] * 2 + [FREE] * 3 + [VMEM] * 3,
        out_specs=[VMEM] * 4,
        scratch_shapes=slot_scratch(modes, width),
        compiler_params=pltpu.CompilerParams(vmem_limit_bytes=28 * MIB),
        cost_estimate=cost(4, modes, width),
        name="slots_first",
    )(offsets, counts, tile, inner, outer, patterns, probe, table)


def second_slots(offsets, counts, sides, ext, totals, keep, send, patterns, probe, table):
    modes, width = probe.shape[1:3]
    margin = sides[0].shape[1]
    side = (2, ext.shape[2], LANES)
    return pl.pallas_call(
        second_kernel,
        out_shape=shapes(totals.shape, keep.shape, send.shape, side, side),
        in_specs=[SMEM] * 2 + [FREE] * 5 + [VMEM] * 6,
        out_specs=[VMEM] * 3 + [FREE] * 2,
        scratch_shapes=[pltpu.VMEM(ext.shape, F32)] + slot_scratch(modes, width),
        input_output_aliases={7: 0, 8: 1, 9: 2},
        compiler_params=pltpu.CompilerParams(vmem_limit_bytes=28 * MIB),
        cost_estimate=cost(4, modes, width),
        name="slots_second",
    )(offsets, counts, *sides, ext, totals, keep, send, patterns, probe, table)


def prepare_kernel(patterns, probe, out, wide, moving):
    wide[...] = probe[...].astype(F32)
    slots, width = patterns.shape[:2]
    mid = width // 2
    source = lax.broadcasted_iota(jnp.int32, (width, width), 0)
    target = lax.broadcasted_iota(jnp.int32, (width, width), 1)
    wanted = jnp.where(target < mid, 2 * target, 2 * target - (width - 1))
    pick = (source == wanted).astype(BF16)

    def one(number, carry):
        value = patterns[number]
        total = None
        for _ in range(2):
            part = value.astype(BF16)
            value = value - part.astype(F32)
            moved = dot(part, pick)
            total = moved if total is None else total + moved
        for side in range(2):
            lanes = pl.ds(side * mid, mid)
            moving[side] = total[:, side * mid : side * mid + mid]
            for parity in range(2):
                out[number, pl.ds(parity * mid, mid), lanes] = moving[side, pl.ds(parity, mid, 2), :]
        return carry

    lax.fori_loop(0, slots, one, 0)


def prepare(patterns, probe):
    return pl.pallas_call(
        prepare_kernel,
        out_shape=shapes(patterns.shape, probe.shape),
        in_specs=[VMEM] * 2,
        out_specs=[VMEM] * 2,
        scratch_shapes=[pltpu.VMEM((2, patterns.shape[1], patterns.shape[2] // 2), F32)],
        compiler_params=pltpu.CompilerParams(vmem_limit_bytes=12 * MIB),
        cost_estimate=pl.CostEstimate(
            flops=patterns.size * 256 * 6, bytes_accessed=9 * MIB, transcendentals=0
        ),
        name="prepare",
    )(patterns, probe)


def odd_row():
    return lax.rem(lax.axis_index(ROW), 2)


def cut_kernel(tile, near, far, inner, outer, sems):
    margin = near.shape[1]
    rows, cols = tile.shape[1:]
    core = lax.axis_index(CORE)
    odd = odd_row()

    def band(start):
        return tile.at[:, pl.ds(pl.multiple_of(start, LANES), margin), :]

    def strip(start):
        return tile.at[:, :, pl.ds(pl.multiple_of(start, LANES), margin)]

    moves = Moves(sems)
    moves.begin(band((1 - odd) * (rows - margin)), near)
    moves.begin(band(odd * (rows - margin)), far)
    moves.begin(strip(core * (cols - margin)), outer)
    moves.begin(strip((1 - core) * (cols - margin)), inner)
    moves.wait()


def cut(tile, margin):
    rows, cols = tile.shape[1:]
    return pl.pallas_call(
        cut_kernel,
        out_shape=shapes((2, margin, cols), (2, margin, cols), (2, rows, margin), (2, rows, margin)),
        in_specs=[FREE],
        out_specs=[FREE] * 4,
        scratch_shapes=[pltpu.SemaphoreType.DMA((4,))],
        compiler_params=pltpu.CompilerParams(vmem_limit_bytes=MIB),
        cost_estimate=pl.CostEstimate(flops=0, bytes_accessed=4 * MIB, transcendentals=0),
        name="cut",
    )(tile)


def pair_kernel(keep, received, out, total, sems):
    sign = jnp.where(lax.axis_index(CORE) == 0, -1.0, 1.0).astype(F32)
    moves = Moves(sems)
    for k in range(keep.shape[0]):
        total[k] = keep[k] + received[k] * sign
        moves.begin(total.at[k], out.at[k])
    moves.wait()


def pair_sum(keep, received):
    return pl.pallas_call(
        pair_kernel,
        out_shape=jax.ShapeDtypeStruct(keep.shape, F32),
        in_specs=[VMEM] * 2,
        out_specs=FREE,
        scratch_shapes=[pltpu.VMEM(keep.shape, F32), pltpu.SemaphoreType.DMA((keep.shape[0],))],
        compiler_params=pltpu.CompilerParams(vmem_limit_bytes=8 * MIB),
        cost_estimate=pl.CostEstimate(flops=600_000, bytes_accessed=3 * MIB, transcendentals=0),
        name="pair_sum",
    )(keep, received)


def stash_kernel(totals, out, sems):
    rows = pl.ds(0, totals.shape[2])
    moves = Moves(sems)
    for j in range(totals.shape[1] - 2):
        moves.begin(totals.at[:, 1 + j], out.at[:, rows, pl.ds(j * LANES, LANES)])
    moves.wait()


def stash(totals):
    planes, blocks, rows, lanes = totals.shape
    return pl.pallas_call(
        stash_kernel,
        out_shape=jax.ShapeDtypeStruct((planes, SPARE * rows, (blocks - 2) * lanes), F32),
        in_specs=[VMEM],
        out_specs=FREE,
        scratch_shapes=[pltpu.SemaphoreType.DMA((blocks,))],
        compiler_params=pltpu.CompilerParams(vmem_limit_bytes=6 * MIB),
        cost_estimate=pl.CostEstimate(flops=0, bytes_accessed=6 * MIB, transcendentals=0),
        name="stash",
    )(totals)


def corners_kernel(inner, outer, near, far, sems):
    margin = near.shape[1]
    start = inner.shape[1] - margin
    odd = odd_row()
    moves = Moves(sems)
    for target, begin in ((near, (1 - odd) * start), (far, odd * start)):
        rows = pl.ds(pl.multiple_of(begin, LANES), margin)
        moves.begin(inner.at[:, rows, :], target.at[:, :, pl.ds(0, LANES)])
        moves.begin(outer.at[:, rows, :], target.at[:, :, pl.ds(LANES, LANES)])
    moves.wait()


def corners(inner, outer):
    shape = (2, inner.shape[2], 2 * LANES)
    return pl.pallas_call(
        corners_kernel,
        out_shape=shapes(shape, shape),
        in_specs=[FREE] * 2,
        out_specs=[FREE] * 2,
        scratch_shapes=[pltpu.SemaphoreType.DMA((4,))],
        compiler_params=pltpu.CompilerParams(vmem_limit_bytes=MIB),
        cost_estimate=pl.CostEstimate(flops=0, bytes_accessed=MIB, transcendentals=0),
        name="corners",
    )(inner, outer)


def add_sides(add, inner, outer, last):
    core = lax.axis_index(CORE)

    @pl.when(core == 0)
    def _():
        add(outer, 0)
        add(inner, last)

    @pl.when(core != 0)
    def _():
        add(inner, 0)
        add(outer, last)


def spread_kernel(grown, inner_in, outer_in, near_out, far_out, strips, inner, outer, sems):
    margin, cols = strips.shape[2:]
    low, high = pl.ds(0, margin), pl.ds(inner_in.shape[1] - margin, margin)
    first = Moves(sems)
    for side_in, side in ((inner_in, inner), (outer_in, outer)):
        first.begin(side_in.at[:, low, :], side.at[:, low, :])
        first.begin(side_in.at[:, high, :], side.at[:, pl.ds(margin, margin), :])
    first.begin(grown.at[:, low, :], strips.at[0])
    first.begin(grown.at[:, high, :], strips.at[1])
    first.wait()
    last = Moves(sems)

    def add(side, start):
        lanes = pl.ds(start, LANES)
        strips[0, :, :, lanes] += side[:, :margin, :]
        strips[1, :, :, lanes] += side[:, margin:, :]

    add_sides(add, inner, outer, cols - LANES)
    odd = odd_row()
    last.begin(strips.at[1 - odd], near_out)
    last.begin(strips.at[odd], far_out)
    last.wait()


def spread(grown, inner, outer):
    margin = inner.shape[2]
    strip, ends = (2, margin, grown.shape[2]), (2, 2 * margin, margin)
    return pl.pallas_call(
        spread_kernel,
        out_shape=shapes(strip, strip),
        in_specs=[FREE] * 3,
        out_specs=[FREE] * 2,
        scratch_shapes=[pltpu.VMEM(x, F32) for x in ((2,) + strip, ends, ends)]
        + [pltpu.SemaphoreType.DMA((6,))],
        compiler_params=pltpu.CompilerParams(vmem_limit_bytes=6 * MIB),
        cost_estimate=pl.CostEstimate(flops=600_000, bytes_accessed=4 * MIB, transcendentals=0),
        name="spread",
    )(grown, inner, outer)


def fold_kernel(pieces, copies_out, copies, sems):
    count = pieces.shape[0]
    total = pieces[0]
    for n in range(1, count):
        total = total + pieces[n]
    moves = Moves(sems)
    part = count // 4
    for q in range(4):
        for n in range(part):
            copies[q * part + n] = total
        span = pl.ds(q * part, part)
        moves.begin(copies.at[span], copies_out.at[span])
    moves.wait()


def fold(pieces):
    return pl.pallas_call(
        fold_kernel,
        out_shape=jax.ShapeDtypeStruct(pieces.shape, F32),
        in_specs=[VMEM],
        out_specs=FREE,
        scratch_shapes=[pltpu.VMEM(pieces.shape, F32), pltpu.SemaphoreType.DMA((4,))],
        compiler_params=pltpu.CompilerParams(vmem_limit_bytes=4 * MIB),
        cost_estimate=pl.CostEstimate(flops=300_000, bytes_accessed=2 * MIB, transcendentals=0),
        name="fold",
    )(pieces)


def finish_kernel(grown, inner_in, outer_in, near, far, out, center, inner, outer, strips, sems):
    margin = near.shape[1]
    rows, cols = center.shape[1:]
    middle = pl.ds(margin, rows)
    odd = odd_row()
    loads = []
    for p in range(2):
        moves = Moves(sems.at[p])
        moves.begin(grown.at[p, middle, :], center.at[p])
        moves.begin(inner_in.at[p, middle], inner.at[p])
        moves.begin(outer_in.at[p, middle], outer.at[p])
        moves.begin(near.at[p], strips.at[1 - odd, p])
        moves.begin(far.at[p], strips.at[odd, p])
        loads.append(moves)
    stores = Moves(sems.at[2])
    for p in range(2):
        loads[p].wait()
        center[p, :margin, :] += strips[0, p]
        center[p, rows - margin :, :] += strips[1, p]

        def add(side, start):
            center[p, :, pl.ds(start, LANES)] += side[p]

        add_sides(add, inner, outer, cols - LANES)
        stores.begin(center.at[p], out.at[p])
    stores.wait()


def finish(grown, inner, outer, near, far):
    center = (2, inner.shape[1] - 2 * near.shape[1], near.shape[2])
    side = (2, center[1], LANES)
    made = (center, side, side, (2,) + near.shape)
    return pl.pallas_call(
        finish_kernel,
        out_shape=jax.ShapeDtypeStruct(center, F32),
        in_specs=[FREE] * 5,
        out_specs=FREE,
        scratch_shapes=[pltpu.VMEM(x, F32) for x in made] + [pltpu.SemaphoreType.DMA((3, 5))],
        compiler_params=pltpu.CompilerParams(vmem_limit_bytes=8 * MIB),
        cost_estimate=pl.CostEstimate(flops=600_000, bytes_accessed=7 * MIB, transcendentals=0),
        name="finish",
    )(grown, inner, outer, near, far)


def join_kernel(own, other, out, sems):
    core = lax.axis_index(CORE)
    moves = Moves(sems)
    moves.begin(own, out.at[core])
    moves.begin(other, out.at[1 - core])
    moves.wait()


def join(own, other):
    return pl.pallas_call(
        join_kernel,
        out_shape=jax.ShapeDtypeStruct((2,) + own.shape, F32),
        in_specs=[FREE, FREE],
        out_specs=FREE,
        scratch_shapes=[pltpu.SemaphoreType.DMA((2,))],
        compiler_params=pltpu.CompilerParams(vmem_limit_bytes=MIB),
        cost_estimate=pl.CostEstimate(flops=0, bytes_accessed=4 * MIB, transcendentals=0),
        name="join",
    )(own, other)


def swap_inner(block, axes):
    count = lax.axis_size(axes)
    return lax.ppermute(block, axes, [(i, i ^ 1) for i in range(count)])


def swap_outer(block, axes):
    count = lax.axis_size(axes)
    pairs = [(i, i + 1) for i in range(1, count - 1, 2)]
    return lax.ppermute(block, axes, pairs + [(j, i) for i, j in pairs])


def exchange(counts, pieces):
    def send(given):
        return lax.all_to_all(given, CHIP, 0, 0, tiled=True)

    return lax.cond(counts[0, 0] > 0, send, jnp.zeros_like, pieces)


def on_device(object_field, probe, patterns, offsets, counts):
    width = patterns.shape[1]
    modes = probe.shape[1]

    near, far, inner, outer = cut(object_field, width // 2)
    near = swap_inner(near, ROW)
    far = swap_outer(far, ROW)
    outer = swap_outer(outer, COL)
    inner = swap_inner(inner, COL)
    corner_near, corner_far = corners(inner, outer)
    corner_near = swap_inner(corner_near, ROW)
    corner_far = swap_outer(corner_far, ROW)

    table = jnp.asarray(tables(width))
    measured, wide = prepare(patterns, probe)
    ext, totals, keep, send = first_slots(
        offsets, counts, object_field, inner, outer, measured, wide, table
    )
    sides = (near, far, corner_near, corner_far)
    totals, keep, send, inner, outer = second_slots(
        offsets, counts, sides, ext, totals, keep, send, measured, wide, table
    )

    received = swap_inner(send, COL)
    outer = swap_outer(outer, COL)
    inner = swap_inner(inner, COL)
    grown = stash(totals)
    received, grown = lax.optimization_barrier((received, grown))
    pair = pair_sum(keep, received)
    chips = lax.axis_size(CHIP)
    pieces = exchange(counts, pair.reshape(chips, modes * width // chips, width))
    pieces, inner, outer = lax.optimization_barrier((pieces, inner, outer))
    near, far = spread(grown, inner, outer)
    pieces, near, far = lax.optimization_barrier((pieces, near, far))
    near = swap_inner(near, ROW)
    far = swap_outer(far, ROW)
    gathered = exchange(counts, fold(pieces)).reshape(modes, width, width)
    gathered, near, far = lax.optimization_barrier((gathered, near, far))
    other = swap_inner(gathered, COL)
    object_grad = finish(grown, inner, outer, near, far)
    return (object_grad, join(gathered, other))


def solution(mesh):
    rows, cols = mesh.devices.shape
    side = math.isqrt(rows)
    fine = Mesh(mesh.devices.reshape(side, side, cols // 2, 2), CHIP + (CORE,))
    in_specs = (P(None, ROW, COL), P(), P(ROW + COL, None, None), P(None, ROW + COL), P(ROW, COL))
    out_specs = (P(None, ROW, COL), P())
    return jax.shard_map(
        on_device, mesh=fine, in_specs=in_specs, out_specs=out_specs, check_vma=False
    )
```
